512 devices in a mesh: wide: 128 (over z, x, y_lo), narrow: 4 (over y_hi, core).
Axes of the slice: x: 4, y: 4 (y_hi: 2, y_lo: 2; y = y_hi * 2 + y_lo), z: 16, core: 2. Of those that a mesh axis runs over, the one named last changes fastest.
Arguments:
- star_pos: float32 [3, 32768], P(None, ('wide', 'narrow')), may hold values from -6 to 6
- star_vel: float32 [3, 32768], P(None, ('wide', 'narrow')), may hold values from -6 to 6
- star_mass: float32 [32768], P(('wide', 'narrow')), may hold values from 0.00048828125 to 0.0048828125
- star_acc: float32 [3, 32768], P(None, ('wide', 'narrow')), may hold values from -6 to 6
- star_jerk: float32 [3, 32768], P(None, ('wide', 'narrow')), may hold values from -120 to 120
- gal_pos: float32 [3, 262144], P(None, ('wide', 'narrow')), may hold values from -6 to 6
- gal_vel: float32 [3, 262144], P(None, ('wide', 'narrow')), may hold values from -6 to 6
- gal_mass: float32 [262144], P(('wide', 'narrow')), may hold values from 0.0009765625 to 0.009765625
- group_of: int32 [262144], P(('wide', 'narrow')), may hold values from 0 to 31, as said below
- let_send: int32 [512, 128, 1], P(('wide', 'narrow')), may hold values from -1 to 3, as said below
- star_leaf: int32 [2048, 8], P(('wide', 'narrow')), may hold values from 0 to 127, as said below
Outputs:
- gal_vel_new: float32 [3, 262144], P(None, ('wide', 'narrow'))
- star_pos_new: float32 [3, 32768], P(None, ('wide', 'narrow'))
- star_vel_new: float32 [3, 32768], P(None, ('wide', 'narrow'))
The draws below stay inside these ranges and needn't reach their ends.
Inputs may be any that keep to these rules, and one draw needn't show every extreme that they name: `group_of`: within each leaf of 128 bodies every group number is held by exactly 4 bodies. `let_send`: entry [k, j, s] is a local leaf of device k sent to the device of wide index j with k's narrow index, or -1 for an empty slot; the leaves of one row are distinct; a device lists nothing for its own wide index; for some wide index j, every device whose wide index is not j lists a leaf for j, in every draw. `star_leaf`: the star blocks listed for one leaf are distinct.
All inputs are finite; a program needn't handle non-finite values.
Results may differ from the reference program's by a relative error of at most 0.0003.
Values sent between devices are 32-bit elements; how exact they have to be, the bound alone decides.
No kernel may reach another device: no remote copies, remote signals or barrier semaphores. Data moves between devices by JAX's collectives and lax.ppermute only.
A program may use at most 64 MiB of HBM per device.

```python
import math
import jax
import jax.numpy as jnp
from jax import lax

LEAF = 128
GROUPS = 32
L_DEV = 4
S_DEV = 64
SLOTS = 1
KICK_BLOCKS = 8
NS = 32768
NLEAF = 2048
NB = 262144
N_WIDE = 128
N_NARROW = 4
DEVICES = 512


def draw_group_of(key, part):
    keys = jax.random.split(key, NLEAF)
    base = jnp.arange(LEAF, dtype=jnp.int32) % GROUPS
    rows = jax.vmap(lambda row_key: jax.random.permutation(row_key, base))(keys)
    return rows.reshape(NB).astype(jnp.int32)


def draw_let_send(key, part):
    key_perm, key_busy, key_special, key_roll = jax.random.split(jax.random.fold_in(key, 11), 4)
    keys = jax.random.split(key_perm, DEVICES * N_WIDE)
    base = jnp.arange(L_DEV, dtype=jnp.int32)
    picks = jax.vmap(lambda row_key: jax.random.permutation(row_key, base)[:SLOTS])(keys)
    picks = picks.reshape(DEVICES, N_WIDE, SLOTS)
    busy = jax.random.randint(key_busy, (N_WIDE,), 1, 5)
    special = jax.random.randint(key_special, (), 0, N_WIDE)
    busy = jnp.where(jnp.arange(N_WIDE) == special, 4, busy)
    roll = jax.random.randint(key_roll, (DEVICES, N_WIDE, SLOTS), 0, 4)
    live = roll < busy[None, :, None]
    own = (jnp.arange(DEVICES) // N_NARROW)[:, None] == jnp.arange(N_WIDE)[None, :]
    live = jnp.logical_and(live, jnp.logical_not(own)[:, :, None])
    return jnp.where(live, picks, -1).astype(jnp.int32)


def draw_star_leaf(key, part):
    keys = jax.random.split(jax.random.fold_in(key, 23), NLEAF)
    base = jnp.arange(N_WIDE, dtype=jnp.int32)
    rows = jax.vmap(lambda row_key: jax.random.permutation(row_key, base)[:KICK_BLOCKS])(keys)
    return rows.astype(jnp.int32)


def shard_levels(stream_key, shape, cuts, least, top_value):
    level, own = 1.0, jax.random.fold_in(stream_key, 6)
    for position, blocks in cuts:
        steps = jnp.exp(jax.random.uniform(jax.random.fold_in(own, position), (blocks,), jnp.float32, least / len(cuts), top_value / len(cuts)))
        level = level * jnp.repeat(steps, shape[position] // blocks).reshape([-1 if axis == position else 1 for axis in range(len(shape))])
    return level


def bell_draw(rng, shape, width, bound, cuts=(), kind=jnp.bfloat16):
    loudness = shard_levels(rng, shape, cuts, -0.22, 0.18) if cuts else 1.0
    entries = jax.random.normal(rng, shape, jnp.float32) * width * loudness
    return jnp.minimum(jnp.maximum(entries, -bound), bound).astype(kind)


def setup_inputs(seed: int = 0) -> dict:
    streams_of = jax.random.split(jax.random.key(seed), 12)
    star_pos = bell_draw(streams_of[0], (3, NS), 1.0, 6.0, ((1, 512),), jnp.float32)
    star_vel = bell_draw(streams_of[1], (3, NS), 1.0, 6.0, ((1, 512),), jnp.float32)
    star_mass = jnp.clip(jnp.exp(math.log(0.0048828125) - 2.3025851 * jax.random.uniform(streams_of[2], (NS,), jnp.float32) ** shard_levels(streams_of[2], (NS,), ((0, 512),), -0.2, 0.2)), 0.00048828125, 0.0048828125)
    star_acc = bell_draw(streams_of[3], (3, NS), 1.0, 6.0, ((1, 512),), jnp.float32)
    star_jerk = bell_draw(streams_of[4], (3, NS), 20.0, 120.0, ((1, 512),), jnp.float32)
    gal_pos = bell_draw(streams_of[5], (3, NB), 1.0, 6.0, ((1, 512),), jnp.float32)
    gal_vel = bell_draw(streams_of[6], (3, NB), 1.0, 6.0, ((1, 512),), jnp.float32)
    gal_mass = jnp.clip(jnp.exp(math.log(0.009765625) - 2.3025851 * jax.random.uniform(streams_of[7], (NB,), jnp.float32) ** shard_levels(streams_of[7], (NB,), ((0, 512),), -0.2, 0.2)), 0.0009765625, 0.009765625)
    group_of = draw_group_of(jax.random.fold_in(streams_of[11], 71), 0)
    let_send = draw_let_send(jax.random.fold_in(streams_of[11], 71), 0)
    star_leaf = draw_star_leaf(jax.random.fold_in(streams_of[11], 71), 0)
    return {"star_pos": star_pos, "star_vel": star_vel, "star_mass": star_mass, "star_acc": star_acc, "star_jerk": star_jerk, "gal_pos": gal_pos, "gal_vel": gal_vel, "gal_mass": gal_mass, "group_of": group_of, "let_send": let_send, "star_leaf": star_leaf}


time_step = 0.25
soften_sq = 0.05

def by_blocks(kernel, arrays):
    total_rows = arrays[0].shape[1]
    block_rows = math.gcd(total_rows, 512)
    nblocks = total_rows // block_rows
    split = tuple((member.reshape(member.shape[0], nblocks, block_rows).transpose(1, 0, 2) for member in arrays))
    result = lax.map(kernel, split)
    return jax.tree.map(lambda piece: piece.transpose(1, 0, 2).reshape(piece.shape[1], total_rows), result)

def attract(tgt_pos, src_pos, src_mass):

    def kernel(pieces):
        here_pos = pieces[0]
        offset = src_pos[:, None, :] - here_pos[:, :, None]
        dist_sq = lax.optimization_barrier(jnp.sum(offset * offset, axis=0)) + soften_sq
        inverse = lax.rsqrt(dist_sq)
        weight = src_mass[None, :] * inverse * inverse * inverse
        return lax.optimization_barrier(jnp.sum(offset * weight[None], axis=2))
    return by_blocks(kernel, (tgt_pos,))

def hermite(tgt_pos, tgt_vel, src_pos, src_vel, src_mass):

    def kernel(pieces):
        here_pos, here_vel = pieces
        offset = src_pos[:, None, :] - here_pos[:, :, None]
        rel_vel = src_vel[:, None, :] - here_vel[:, :, None]
        dist_sq = lax.optimization_barrier(jnp.sum(offset * offset, axis=0)) + soften_sq
        inverse = lax.rsqrt(dist_sq)
        weight = src_mass[None, :] * inverse * inverse * inverse
        approach = 3.0 * lax.optimization_barrier(jnp.sum(offset * rel_vel, axis=0)) / dist_sq
        accel_sum = lax.optimization_barrier(jnp.sum(offset * weight[None], axis=2))
        jerk_sum = lax.optimization_barrier(jnp.sum((rel_vel - offset * approach[None]) * weight[None], axis=2))
        return (accel_sum, jerk_sum)
    return by_blocks(kernel, (tgt_pos, tgt_vel))

def reference(star_pos, star_vel, star_mass, star_acc, star_jerk, gal_pos, gal_vel, gal_mass, group_of, let_send, star_leaf):
    step_sq = time_step * time_step
    pred_pos = star_pos + time_step * star_vel + step_sq * 0.5 * star_acc + step_sq * time_step / 6.0 * star_jerk
    pred_vel = star_vel + time_step * star_acc + step_sq * 0.5 * star_jerk
    direct_acc, direct_jerk = hermite(pred_pos, pred_vel, pred_pos, pred_vel, star_mass)
    leaf_of = jnp.arange(NB, dtype=jnp.int32) // LEAF
    segment = leaf_of * GROUPS + group_of
    cell_mass = jax.ops.segment_sum(gal_mass, segment, num_segments=NLEAF * GROUPS)
    cell_mom = jax.vmap(lambda coord: jax.ops.segment_sum(coord * gal_mass, segment, num_segments=NLEAF * GROUPS))(gal_pos)
    cell_pos = cell_mom / cell_mass[None]
    local_size = L_DEV * LEAF
    group_range = jnp.arange(GROUPS, dtype=jnp.int32)
    star_range = jnp.arange(S_DEV, dtype=jnp.int32)

    def per_device(device):
        wide_idx = device // N_NARROW
        narrow_idx = device % N_NARROW
        sources = jnp.arange(N_WIDE, dtype=jnp.int32) * N_NARROW + narrow_idx
        slot_ids = let_send[sources, wide_idx]
        live = (slot_ids >= 0).astype(jnp.float32)
        leaf_idx = sources[:, None] * L_DEV + jnp.maximum(slot_ids, 0)
        cell_idx = (leaf_idx[:, :, None] * GROUPS + group_range[None, None, :]).reshape(-1)
        let_pos = cell_pos[:, cell_idx]
        let_mass = (cell_mass[cell_idx].reshape(N_WIDE, SLOTS, GROUPS) * live[:, :, None]).reshape(-1)
        own_cells = device * (L_DEV * GROUPS) + jnp.arange(L_DEV * GROUPS, dtype=jnp.int32)
        cells_pos = jnp.concatenate([cell_pos[:, own_cells], let_pos], axis=1)
        cells_mass = jnp.concatenate([cell_mass[own_cells], let_mass], axis=0)
        start = (device * local_size).astype(jnp.int32)
        bodies = lax.dynamic_slice_in_dim(gal_pos, start, local_size, 1)
        masses = lax.dynamic_slice_in_dim(gal_mass, start, local_size, 0)
        gal_acc = attract(bodies, bodies, masses) + attract(bodies, let_pos, let_mass)
        blocks = lax.dynamic_slice_in_dim(star_leaf, (device * L_DEV).astype(jnp.int32), L_DEV, 0)
        star_idx = (((blocks * N_NARROW + narrow_idx) * S_DEV)[:, :, None] + star_range[None, None, :]).reshape(L_DEV, KICK_BLOCKS * S_DEV)
        leaf_targets = bodies.reshape(3, L_DEV, LEAF)
        star_term = jax.vmap(lambda target, index: attract(target, pred_pos[:, index], star_mass[index]), in_axes=(1, 0), out_axes=1)(leaf_targets, star_idx)
        gal_acc = gal_acc + star_term.reshape(3, local_size)
        own_stars = lax.dynamic_slice_in_dim(pred_pos, (device * S_DEV).astype(jnp.int32), S_DEV, 1)
        star_cell = attract(own_stars, cells_pos, cells_mass)
        return (gal_acc, star_cell)
    gal_acc, cell_acc = lax.map(per_device, jnp.arange(DEVICES, dtype=jnp.int32))
    gal_acc = gal_acc.transpose(1, 0, 2).reshape(3, NB)
    cell_acc = cell_acc.transpose(1, 0, 2).reshape(3, NS)
    gal_vel_new = gal_vel + time_step * gal_acc
    new_acc = direct_acc + cell_acc
    star_vel_new = star_vel + time_step * 0.5 * (star_acc + new_acc) + step_sq / 12.0 * (star_jerk - direct_jerk)
    star_pos_new = star_pos + time_step * 0.5 * (star_vel + star_vel_new) + step_sq / 12.0 * (star_acc - new_acc)
    return (gal_vel_new, star_pos_new, star_vel_new)
```

```python
import functools

import jax
import jax.numpy as jnp
from jax import lax
from jax.experimental import pallas as pl
from jax.experimental.pallas import tpu as pltpu
from jax.sharding import Mesh
from jax.sharding import PartitionSpec as P

GROUPS = 32
LEAF = 128
LANES = 128
TIME_STEP = 0.25
SOFT_SQ = 0.05
STEP_SQ = TIME_STEP * TIME_STEP
HIGHEST = lax.Precision.HIGHEST
F32 = jnp.float32

Z, XY, NARROW = "wide_z", "wide_xy", "narrow"
ALL = (Z, XY, NARROW)
N_Z, N_XY, N_NARROW = 16, 8, 4
STARS = 64
STAR_ROWS = 4


def predict(pos, vel, acc, jerk):
    pred_pos = pos + TIME_STEP * vel + STEP_SQ * 0.5 * acc + STEP_SQ * TIME_STEP / 6.0 * jerk
    pred_vel = vel + TIME_STEP * acc + STEP_SQ * 0.5 * jerk
    return pred_pos, pred_vel


def prepare_kernel(pos, vel, acc, jerk, mass, gpos, gmass, group, let, star_out, cells_out, send_out):
    pred_pos, pred_vel = predict(pos[...], vel[...], acc[...], jerk[...])
    zero = jnp.zeros((1, STARS), F32)
    rows = [
        (pred_pos[0:1], pred_pos[1:2]),
        (pred_pos[2:3], pred_vel[0:1]),
        (pred_vel[1:2], pred_vel[2:3]),
        (mass[...], zero),
    ]
    packed = jnp.concatenate([jnp.concatenate(pair, axis=1) for pair in rows], axis=0)
    packed = jnp.concatenate([packed, jnp.zeros((4, LANES), F32)], axis=0)
    for n in range(N_NARROW):
        star_out[n] = packed
    leaf_rows = []
    for leaf in range(4):
        span = pl.ds(leaf * LEAF, LEAF)
        m = gmass[:, span]
        stacked = jnp.concatenate([gpos[:, span] * m, m, jnp.zeros((4, LEAF), F32)], axis=0)
        onehot = jnp.where(
            lax.broadcasted_iota(jnp.int32, (GROUPS, LEAF), 0) == group[:, span], 1.0, 0.0
        )
        sums = lax.dot_general(
            stacked, onehot, (((1,), (1,)), ((), ())), precision=HIGHEST, preferred_element_type=F32
        )
        total = sums[3:4]
        centre = sums[0:3] / total
        leaf_rows.append(
            jnp.concatenate([centre[0:1], centre[1:2], centre[2:3], total], axis=1)
        )
    cells_out[...] = jnp.concatenate(leaf_rows + [jnp.zeros((4, LANES), F32)], axis=0)
    ids = jnp.broadcast_to(let[...], (N_Z * N_XY, LANES))
    chosen = jnp.zeros((N_Z * N_XY, LANES), F32)
    for leaf in range(4):
        chosen = jnp.where(ids == leaf, jnp.broadcast_to(leaf_rows[leaf], chosen.shape), chosen)
    for z in range(N_Z):
        send_out[z, 0:8] = chosen[8 * z : 8 * z + 8]
        send_out[z, 8:16] = packed


def low_lanes(shape):
    return lax.broadcasted_iota(jnp.int32, shape, 1) < 64


def star_planes(stars, planes, count):
    half = N_XY // 2 * N_Z
    low = low_lanes((half, LANES))
    for r in range((count + 1) // 2):
        picked = [stars[e, pl.ds(r, N_Z, stride=STAR_ROWS), :] for e in range(N_XY)]
        first = jnp.concatenate(picked[: N_XY // 2], axis=0)
        second = jnp.concatenate(picked[N_XY // 2 :], axis=0)
        planes[2 * r] = jnp.where(low, first, pltpu.roll(second, 64, 1))
        if 2 * r + 1 < count:
            planes[2 * r + 1] = jnp.where(low, pltpu.roll(first, 64, 1), second)


def row_sums(x):
    return lax.dot_general(
        jnp.ones((8, LANES), F32), x, (((1,), (1,)), ((), ())), precision=HIGHEST, preferred_element_type=F32
    )


def hermite_kernel(sib, stars, out, planes, tgt, sums):
    star_planes(stars, planes, 7)
    for n in range(N_NARROW):
        turned = jnp.transpose(sib[n])
        for c in range(6):
            col = turned[64 * (c % 2) : 64 * (c % 2) + 64, c // 2 : c // 2 + 1]
            tgt[c, n * STARS : (n + 1) * STARS] = jnp.broadcast_to(col, (STARS, LANES))
    chunk = 16
    n_rows = planes.shape[1]

    @pl.loop(0, N_NARROW * STARS // chunk)
    def _(i):
        at = pl.ds(pl.multiple_of(i * chunk, chunk), chunk)
        px, py, pz, vx, vy, vz = [tgt[c, at, :] for c in range(6)]

        def step(r, carry):
            ax, ay, az, jx, jy, jz = carry
            qx, qy, qz, ux, uy, uz, m = [
                jnp.broadcast_to(planes[c, pl.ds(r, 1), :], (chunk, LANES)) for c in range(7)
            ]
            dx, dy, dz = qx - px, qy - py, qz - pz
            du, dv, dw = ux - vx, uy - vy, uz - vz
            dist = dx * dx + dy * dy + dz * dz + SOFT_SQ
            inv = lax.rsqrt(dist)
            inv2 = inv * inv
            w = m * inv * inv2
            far = (dx * du + dy * dv + dz * dw) * inv2 * 3.0
            wf = w * far
            return (
                ax + w * dx,
                ay + w * dy,
                az + w * dz,
                jx + (w * du - wf * dx),
                jy + (w * dv - wf * dy),
                jz + (w * dw - wf * dz),
            )

        zero = jnp.zeros((chunk, LANES), F32)
        res = lax.fori_loop(0, n_rows, step, (zero,) * 6, unroll=4)
        for c in range(6):
            sums[c, at, :] = res[c]

    for c in range(6):
        row = row_sums(sums[c])[0:1]
        for n in range(N_NARROW):
            out[n, c : c + 1, 0:STARS] = row[:, n * STARS : (n + 1) * STARS]


def pull_kernel(
    leaf_ref, gpos, gvel, gmass, stars, own, cells, gal_out, cell_out, planes, splanes, cplanes, tgt, stgt, sums
):
    quarter = N_XY // 4
    lane_group = lax.broadcasted_iota(jnp.int32, (32, LANES), 1) // GROUPS
    parts = [
        jnp.concatenate([stars[e, 64:80, :] for e in range(quarter * k, quarter * (k + 1))], axis=0)
        for k in range(4)
    ]
    for c in range(4):
        plane = parts[c]
        for k in range(4):
            if k != c:
                plane = jnp.where(lane_group == k, pltpu.roll(parts[k], (GROUPS * (k - c)) % LANES, 1), plane)
        planes[c, 0:32] = plane
    one_group = lax.broadcasted_iota(jnp.int32, (1, LANES), 1) // GROUPS
    for c in range(4):
        row = cells[c : c + 1]
        for k in range(4):
            if k != c:
                row = jnp.where(one_group == k, pltpu.roll(cells[k : k + 1], (GROUPS * (k - c)) % LANES, 1), row)
        cplanes[c : c + 1] = row
    for leaf in range(4):
        span = pl.ds(leaf * LEAF, LEAF)
        for c in range(3):
            planes[c, 32 + leaf : 33 + leaf] = gpos[c : c + 1, span]
        planes[3, 32 + leaf : 33 + leaf] = gmass[:, span]
    star_planes(stars, splanes, 7)
    low = low_lanes((1, LANES))
    for leaf in range(4):
        for pair in range(4):
            picks = []
            for side in range(2):
                b = leaf_ref[leaf, 2 * pair + side]
                place = (b % N_XY) * N_Z + b // N_XY
                upper = place // 64
                picks.append((place - 64 * upper, upper))
            for c in range(4):
                plane = c if c < 3 else 6
                sides = []
                for side in range(2):
                    at, upper = picks[side]
                    row = splanes[plane, pl.ds(at, 1), :]
                    sides.append(jnp.where(upper == side, row, pltpu.roll(row, 64, 1)))
                planes[c, 36 + 4 * leaf + pair : 37 + 4 * leaf + pair] = jnp.where(low, sides[0], sides[1])
    for leaf in range(4):
        span = pl.ds(leaf * LEAF, LEAF)
        block = jnp.concatenate([gpos[:, span], jnp.zeros((5, LEAF), F32)], axis=0)
        turned = jnp.transpose(block)
        for c in range(3):
            tgt[c, leaf * LEAF : (leaf + 1) * LEAF] = jnp.broadcast_to(turned[:, c : c + 1], (LEAF, LANES))
    turned = jnp.transpose(own[...])
    for c in range(3):
        stgt[c] = jnp.broadcast_to(
            turned[64 * (c % 2) : 64 * (c % 2) + 64, c // 2 : c // 2 + 1], (STARS, LANES)
        )
    chunk = 32

    def add_pull(source, here, total):
        dx, dy, dz = [jnp.broadcast_to(source[c], here[c].shape) - here[c] for c in range(3)]
        inv = lax.rsqrt(dx * dx + dy * dy + dz * dz + SOFT_SQ)
        w = jnp.broadcast_to(source[3], here[0].shape) * inv * (inv * inv)
        return total[0] + w * dx, total[1] + w * dy, total[2] + w * dz

    def source_at(r):
        return [planes[c, pl.ds(r, 1), :] for c in range(4)]

    zero = jnp.zeros((chunk, LANES), F32)

    @pl.loop(0, 4 * LEAF // chunk)
    def _(i):
        at = pl.ds(pl.multiple_of(i * chunk, chunk), chunk)
        here = [tgt[c, at, :] for c in range(3)]
        res = lax.fori_loop(0, 36, lambda r, t: add_pull(source_at(r), here, t), (zero,) * 3, unroll=4)
        first = 36 + 4 * (i // (LEAF // chunk))
        for k in range(4):
            res = add_pull(source_at(first + k), here, res)
        for c in range(3):
            sums[c, at, :] = res[c]

    for c in range(3):
        gal_out[c : c + 1] = gvel[c : c + 1] + TIME_STEP * row_sums(sums[c])[0:1]

    for i in range(STARS // chunk):
        here = [stgt[c, i * chunk : (i + 1) * chunk, :] for c in range(3)]
        res = lax.fori_loop(0, 32, lambda r, t: add_pull(source_at(r), here, t), (zero,) * 3, unroll=4)
        res = add_pull([cplanes[c : c + 1] for c in range(4)], here, res)
        for c in range(3):
            sums[c, i * chunk : (i + 1) * chunk, :] = res[c]
    for c in range(3):
        cell_out[c : c + 1, 0:STARS] = row_sums(sums[c, 0:STARS])[0:1]


def correct_kernel(pos, vel, acc, jerk, parts, cell, pos_out, vel_out):
    summed = parts[0] + parts[1] + parts[2] + parts[3]
    new_acc = summed[0:3, 0:STARS] + cell[0:3, 0:STARS]
    new_jerk = summed[3:6, 0:STARS]
    new_vel = (
        vel[...]
        + TIME_STEP * 0.5 * (acc[...] + new_acc)
        + STEP_SQ / 12.0 * (jerk[...] - new_jerk)
    )
    vel_out[...] = new_vel
    pos_out[...] = (
        pos[...]
        + TIME_STEP * 0.5 * (vel[...] + new_vel)
        + STEP_SQ / 12.0 * (acc[...] - new_acc)
    )


def shape(*lengths):
    return jax.ShapeDtypeStruct(lengths, F32)


VMEM_SPEC = pl.BlockSpec(memory_space=pltpu.VMEM)
PARAMS = pltpu.CompilerParams(vmem_limit_bytes=32 * 1024 * 1024)


def body(
    star_pos, star_vel, star_mass, star_acc, star_jerk, gal_pos, gal_vel, gal_mass, group_of, let_send, star_leaf
):
    star_rows, cells, send = pl.pallas_call(
        prepare_kernel,
        out_shape=(shape(N_NARROW, 8, LANES), shape(8, LANES), shape(N_Z, 16, LANES)),
        in_specs=[VMEM_SPEC] * 9,
        out_specs=(VMEM_SPEC,) * 3,
        compiler_params=PARAMS,
    )(
        star_pos,
        star_vel,
        star_acc,
        star_jerk,
        star_mass.reshape(1, -1),
        gal_pos,
        gal_mass.reshape(1, -1),
        group_of.reshape(1, -1),
        let_send.reshape(-1, 1),
    )
    arrived = lax.all_to_all(send, Z, split_axis=0, concat_axis=0, tiled=True)
    siblings = lax.all_to_all(star_rows, NARROW, split_axis=0, concat_axis=0, tiled=True)
    star_part = arrived[:, 8:12].reshape(1, N_Z * STAR_ROWS, LANES)
    cell_part = arrived[:, 0:8].transpose(1, 0, 2)
    onward = jnp.concatenate(
        [jnp.broadcast_to(star_part, (N_XY, *star_part.shape[1:])), cell_part], axis=1
    )
    stars = lax.all_to_all(onward, XY, split_axis=0, concat_axis=0, tiled=True)
    partial = pl.pallas_call(
        hermite_kernel,
        out_shape=shape(N_NARROW, 8, LANES),
        in_specs=[VMEM_SPEC] * 2,
        out_specs=VMEM_SPEC,
        scratch_shapes=[
            pltpu.VMEM((7, 64, LANES), F32),
            pltpu.VMEM((6, N_NARROW * STARS, LANES), F32),
            pltpu.VMEM((6, N_NARROW * STARS, LANES), F32),
        ],
        compiler_params=PARAMS,
        cost_estimate=pl.CostEstimate(flops=80_000_000, bytes_accessed=400_000, transcendentals=2_000_000),
    )(siblings, stars)
    shared = lax.all_to_all(partial, NARROW, split_axis=0, concat_axis=0, tiled=True)
    gal_vel_new, cell_acc = pl.pallas_call(
        pull_kernel,
        out_shape=(shape(3, 4 * LEAF), shape(8, LANES)),
        in_specs=[pl.BlockSpec(memory_space=pltpu.SMEM)] + [VMEM_SPEC] * 6,
        out_specs=(VMEM_SPEC,) * 2,
        scratch_shapes=[
            pltpu.VMEM((4, 56, LANES), F32),
            pltpu.VMEM((7, 64, LANES), F32),
            pltpu.VMEM((8, LANES), F32),
            pltpu.VMEM((3, 4 * LEAF, LANES), F32),
            pltpu.VMEM((3, STARS, LANES), F32),
            pltpu.VMEM((3, 4 * LEAF, LANES), F32),
        ],
        compiler_params=PARAMS,
        cost_estimate=pl.CostEstimate(flops=60_000_000, bytes_accessed=400_000, transcendentals=3_000_000),
    )(star_leaf, gal_pos, gal_vel, gal_mass.reshape(1, -1), stars, star_rows[0], cells)
    star_pos_new, star_vel_new = pl.pallas_call(
        correct_kernel,
        out_shape=(shape(3, STARS), shape(3, STARS)),
        in_specs=[VMEM_SPEC] * 6,
        out_specs=(VMEM_SPEC,) * 2,
        compiler_params=PARAMS,
    )(star_pos, star_vel, star_acc, star_jerk, shared, cell_acc)
    return gal_vel_new, star_pos_new, star_vel_new


def solution(mesh):
    torus = Mesh(mesh.devices.reshape(N_Z, N_XY, N_NARROW), ALL)
    cols = P(None, ALL)
    return jax.shard_map(
        body,
        mesh=torus,
        in_specs=(
            cols,
            cols,
            P(ALL),
            cols,
            cols,
            cols,
            cols,
            P(ALL),
            P(ALL),
            P(ALL, None, None),
            P(ALL, None),
        ),
        out_specs=(cols, cols, cols),
        check_vma=False,
    )
```

```python
import jax
import jax.numpy as jnp
from jax import lax
from jax.experimental import pallas as pl
from jax.experimental.pallas import tpu as pltpu
from jax.sharding import Mesh
from jax.sharding import PartitionSpec as P

GROUPS = 32
LEAF = 128
LANES = 128
TIME_STEP = 0.25
SOFT_SQ = 0.05
STEP_SQ = TIME_STEP * TIME_STEP
HIGHEST = lax.Precision.HIGHEST
F32, BF16 = jnp.float32, jnp.bfloat16
LANE_BY_LANE = (((1,), (1,)), ((), ()))

Z, XY, NARROW = "wide_z", "wide_xy", "narrow"
ALL = (Z, XY, NARROW)
N_Z, N_XY, N_NARROW = 16, 8, 4
STARS = 64
STAR_ROWS = 4
PER_BLOCK = 2 * LANES


def predict(pos, vel, acc, jerk):
    pred_pos = pos + TIME_STEP * vel + STEP_SQ * 0.5 * acc + STEP_SQ * TIME_STEP / 6.0 * jerk
    pred_vel = vel + TIME_STEP * acc + STEP_SQ * 0.5 * jerk
    return pred_pos, pred_vel


def prepare_kernel(pos, vel, acc, jerk, mass, gpos, gmass, group, let, star_out, own_out, cells_out, send_out):
    pred_pos, pred_vel = predict(pos[...], vel[...], acc[...], jerk[...])
    zero = jnp.zeros((1, STARS), F32)
    rows = [
        (pred_pos[0:1], pred_pos[1:2]),
        (pred_pos[2:3], pred_vel[0:1]),
        (pred_vel[1:2], pred_vel[2:3]),
        (mass[...], zero),
    ]
    packed = jnp.concatenate([jnp.concatenate(pair, axis=1) for pair in rows], axis=0)
    own = jnp.concatenate([packed, jnp.zeros((4, LANES), F32)], axis=0)
    own_out[...] = own
    for n in range(N_NARROW):
        star_out[n] = own
    leaf_rows = []
    for leaf in range(4):
        span = pl.ds(leaf * LEAF, LEAF)
        m = gmass[:, span]
        stacked = jnp.concatenate([gpos[:, span] * m, m, jnp.zeros((4, LEAF), F32)], axis=0)
        onehot = jnp.where(
            lax.broadcasted_iota(jnp.int32, (GROUPS, LEAF), 0) == group[:, span], 1.0, 0.0
        )
        sums = lax.dot_general(stacked, onehot, LANE_BY_LANE, precision=HIGHEST, preferred_element_type=F32)
        total = sums[3:4]
        centre = sums[0:3] / total
        leaf_rows.append(
            jnp.concatenate([centre[0:1], centre[1:2], centre[2:3], total], axis=1)
        )
    cells_out[...] = jnp.concatenate(leaf_rows + [jnp.zeros((4, LANES), F32)], axis=0)
    ids = let[...].astype(F32)
    lane = lax.broadcasted_iota(jnp.int32, (1, LANES), 1)
    listed = jnp.logical_and(lane >= 64, lane < 64 + N_XY)
    for z in range(N_Z):
        turned = pltpu.roll(ids, (64 - N_XY * z) % LANES, 1)
        last = jnp.where(listed, turned, packed[3:4])
        send_out[z] = jnp.concatenate([packed[0:3], last] + leaf_rows, axis=0)


def onward_kernel(arrived, out):
    flat = arrived
    for pair in range(N_Z // 2):
        both = jnp.concatenate(
            [flat[16 * pair : 16 * pair + 4, :], flat[16 * pair + 8 : 16 * pair + 12, :]], axis=0
        )
        for e in range(N_XY):
            out[e, 8 * pair : 8 * pair + 8, :] = both
    ids = flat[pl.ds(3, N_Z, stride=8), :]
    cells = [flat[pl.ds(4 + leaf, N_Z, stride=8), :] for leaf in range(4)]
    for e in range(N_XY):
        which = jnp.broadcast_to(ids[:, 64 + e : 65 + e], (N_Z, LANES))
        rows = jnp.zeros((N_Z, LANES), F32)
        for leaf in range(4):
            rows = jnp.where(which == float(leaf), cells[leaf], rows)
        out[e, 64:80, :] = rows


def low_lanes(shape):
    return lax.broadcasted_iota(jnp.int32, shape, 1) < 64


def star_plane_pair(stars, r):
    low = low_lanes((N_XY // 2 * N_Z, LANES))
    picked = [stars[e, pl.ds(r, N_Z, stride=STAR_ROWS), :] for e in range(N_XY)]
    first = jnp.concatenate(picked[: N_XY // 2], axis=0)
    second = jnp.concatenate(picked[N_XY // 2 :], axis=0)
    return (
        jnp.where(low, first, pltpu.roll(second, 64, 1)),
        jnp.where(low, pltpu.roll(first, 64, 1), second),
    )


def row_sums(x):
    ones = jnp.ones((8, LANES), F32)
    return lax.dot_general(ones, x, LANE_BY_LANE, precision=HIGHEST, preferred_element_type=F32)[0:1]


def split3(x):
    high = x.astype(BF16).astype(F32)
    rest = x - high
    middle = rest.astype(BF16).astype(F32)
    return high, middle, rest - middle


def source_slots(x):
    h, m, l = split3(x)
    none = jnp.zeros_like(x)
    return jnp.concatenate([h, h, h, m, m, l, none, none], axis=0).astype(BF16)


def target_slots(x):
    h, m, l = split3(x)
    rows = jnp.concatenate([h, m, l, h, m, h] + [jnp.zeros_like(x)] * 10, axis=0)
    return jnp.transpose(rows)[:, 0:64].astype(BF16)


def weighted(source, weight):
    h, m, l = split3(source)
    parts = jnp.concatenate([h, m, l, jnp.zeros_like(source)], axis=0).astype(BF16)
    high = weight.astype(BF16)
    low = (weight - high.astype(F32)).astype(BF16)
    return lax.dot_general(parts, high, LANE_BY_LANE, preferred_element_type=F32) + lax.dot_general(
        parts, low, LANE_BY_LANE, preferred_element_type=F32
    )


def add_parts(x):
    return x[0:8] + x[8:16] + x[16:24]


def twice(x):
    return jnp.concatenate([x, x], axis=1)


def store_rows(ref, stride, row, plane):
    blocks = plane.shape[0] // 2
    ref[0, pl.ds(row, blocks, stride=stride), :] = plane[:blocks]
    ref[1, pl.ds(row, blocks, stride=stride), :] = plane[blocks:]


def load_block(ref, at):
    return jnp.concatenate([ref[half, pl.ds(at, 8), :] for half in range(2)], axis=1)


def hermite_kernel(sib, stars, out, table, slots, here, main, drag):
    n_targets = N_NARROW * STARS
    x, y = star_plane_pair(stars, 0)
    z, u = star_plane_pair(stars, 1)
    v, w = star_plane_pair(stars, 2)
    m, _ = star_plane_pair(stars, 3)
    product = m * (x * u + y * v + z * w)
    for row, plane in enumerate((x, y, z)):
        store_rows(table, 16, row, plane)
    for row, plane in enumerate((m * x, m * y, m * z, m * u, m * v, m * w, m, product)):
        store_rows(table, 16, 8 + row, plane)
    comps = [[] for _ in range(6)]
    for n in range(N_NARROW):
        block = sib[n]
        for c in range(6):
            comps[c].append(block[c // 2 : c // 2 + 1, 64 * (c % 2) : 64 * (c % 2) + 64])
    rows = [jnp.concatenate(parts, axis=1) for parts in comps]
    p = jnp.concatenate(rows[0:3], axis=0)
    q = jnp.concatenate(rows[3:6], axis=0)
    own_product = jnp.sum(p * q, axis=0, keepdims=True)
    slots[...] = target_slots(
        jnp.concatenate([-q, -p, own_product, jnp.ones((1, n_targets), F32)], axis=0)
    )
    turned = jnp.transpose(jnp.concatenate([p, jnp.zeros((5, n_targets), F32)], axis=0))
    for c in range(3):
        here[c] = jnp.broadcast_to(turned[:, c : c + 1], (n_targets, LANES))
    main[...] = jnp.zeros(main.shape, F32)
    drag[...] = jnp.zeros(drag.shape, F32)

    def block(b, _):
        at = pl.multiple_of(b * 16, 16)
        g = load_block(table, at)
        s = load_block(table, at + 8)
        dx, dy, dz = [g[c : c + 1] - twice(here[c]) for c in range(3)]
        inv = lax.rsqrt(dx * dx + (dy * dy + (dz * dz + SOFT_SQ)))
        approach = jnp.dot(slots[...], source_slots(s), preferred_element_type=F32)
        inv2 = inv * inv
        weight = inv * inv2
        main[...] += weighted(s, weight)
        pulled = weight * inv2 * approach
        for c, d in enumerate((dx, dy, dz)):
            term = pulled * d
            drag[c] += term[:, 0:LANES] + term[:, LANES:PER_BLOCK]
        return 0

    lax.fori_loop(0, table.shape[1] // 16, block, 0, unroll=4)
    total = add_parts(main[...])
    accel = total[0:3] - p * total[6:7]
    dragged = jnp.concatenate([row_sums(drag[c]) for c in range(3)], axis=0)
    jerk = total[3:6] - q * total[6:7] - 3.0 * dragged
    both = jnp.concatenate([accel, jerk, jnp.zeros((2, n_targets), F32)], axis=0)
    for n in range(N_NARROW):
        out[n, :, 0:STARS] = both[:, n * STARS : (n + 1) * STARS]


CELL_BLOCKS = 16
BODY_BLOCK = 16
STAR_BLOCK = 18
BLOCKS = 26


def by_group(picked):
    lane_group = lax.broadcasted_iota(jnp.int32, picked[0].shape, 1) // GROUPS
    out = []
    for c in range(4):
        plane = picked[c]
        for k in range(4):
            if k != c:
                plane = jnp.where(lane_group == k, pltpu.roll(picked[k], (GROUPS * (k - c)) % LANES, 1), plane)
        out.append(plane)
    return out


def table_rows(x, y, z, m):
    return (x, y, z, m * x, m * y, m * z, m)


def build_table(leaf_ref, gpos, gmass, stars, table, splanes):
    quarter = N_XY // 4
    parts = [
        jnp.concatenate([stars[e, 64:80, :] for e in range(quarter * k, quarter * (k + 1))], axis=0)
        for k in range(4)
    ]
    for row, plane in enumerate(table_rows(*by_group(parts))):
        store_rows(table, 8, row, plane)
    for half in range(2):
        spot = slice(8 * (BODY_BLOCK + half), 8 * (BODY_BLOCK + half) + 7)
        for side in range(2):
            span = slice(half * PER_BLOCK + side * LANES, half * PER_BLOCK + (side + 1) * LANES)
            m = gmass[:, span]
            table[side, spot, :] = jnp.concatenate([gpos[:, span], gpos[:, span] * m, m], axis=0)
    x, y = star_plane_pair(stars, 0)
    z, _ = star_plane_pair(stars, 1)
    m, _ = star_plane_pair(stars, 3)
    for c, plane in enumerate((x, y, z, m)):
        splanes[pl.ds(c, 64, stride=8), :] = plane
    low = low_lanes((8, LANES))
    for leaf in range(4):
        for pair in range(4):
            sides = []
            for side in range(2):
                b = leaf_ref[leaf, 2 * pair + side]
                place = (b % N_XY) * N_Z + b // N_XY
                upper = place // 64
                rows = splanes[pl.ds(pl.multiple_of((place - 64 * upper) * 8, 8), 8), :]
                sides.append(jnp.where(upper == side, rows, pltpu.roll(rows, 64, 1)))
            rows = jnp.where(low, sides[0], sides[1])
            m = rows[3:4]
            first = 8 * (STAR_BLOCK + 2 * leaf + pair // 2)
            table[pair % 2, first : first + 7, :] = jnp.concatenate(
                [rows[0:3], rows[0:3] * m, m], axis=0
            )


def pull_of(block, here):
    dx, dy, dz = [block[c : c + 1] - here[c] for c in range(3)]
    inv = lax.rsqrt(dx * dx + (dy * dy + (dz * dz + SOFT_SQ)))
    return weighted(block, inv * (inv * inv))


def pull_leaves(first, gpos, gvel, table, here, total, gal_out):
    count = 2 * LEAF
    span = slice(first * LEAF, first * LEAF + count)
    p = gpos[:, span]
    turned = jnp.transpose(jnp.concatenate([p, jnp.zeros((5, count), F32)], axis=0))
    for c in range(3):
        here[c, 0:count] = jnp.broadcast_to(turned[:, c : c + 1], (count, LANES))
    total[...] = jnp.zeros(total.shape, F32)

    def block(b, _):
        g = load_block(table, pl.multiple_of(b * 8, 8))
        total[...] += pull_of(g, [twice(here[c, 0:count]) for c in range(3)])
        return 0

    lax.fori_loop(0, STAR_BLOCK, block, 0, unroll=3)
    for k in range(2):
        lanes = slice(k * LEAF, (k + 1) * LEAF)
        for half in range(2):
            at = 8 * (STAR_BLOCK + 2 * (first + k) + half)
            total[:, lanes] += pull_of(load_block(table, at), [twice(here[c, lanes]) for c in range(3)])
    summed = add_parts(total[...])
    gal_out[...] = gvel[:, span] + TIME_STEP * (summed[3:6] - p * summed[6:7])


def first_pull_kernel(leaf_ref, gpos, gvel, gmass, stars, gal_out, table, splanes, here, total):
    table[...] = jnp.zeros(table.shape, F32)
    splanes[...] = jnp.zeros(splanes.shape, F32)
    build_table(leaf_ref, gpos, gmass, stars, table, splanes)
    pull_leaves(0, gpos, gvel, table, here, total, gal_out)


def second_pull_kernel(gpos, gvel, own, cells, table, gal_out, cell_out, here, total, star_total):
    pull_leaves(2, gpos, gvel, table, here, total, gal_out)
    turned = jnp.transpose(own[...])
    for c in range(3):
        column = turned[64 * (c % 2) : 64 * (c % 2) + 64, c // 2 : c // 2 + 1]
        here[c, 0:STARS] = jnp.broadcast_to(column, (STARS, LANES))
    star_total[...] = jnp.zeros(star_total.shape, F32)

    def block(b, _):
        g = load_block(table, pl.multiple_of(b * 8, 8))
        star_total[:, 0:STARS] += pull_of(g, [twice(here[c, 0:STARS]) for c in range(3)])
        return 0

    lax.fori_loop(0, CELL_BLOCKS, block, 0, unroll=4)
    mine = by_group([cells[k : k + 1] for k in range(4)])
    g = jnp.concatenate([*table_rows(*mine), jnp.zeros((1, LANES), F32)], axis=0)
    star_total[:, 0:STARS] += pull_of(g, [here[c, 0:STARS] for c in range(3)])
    summed = add_parts(star_total[:, 0:STARS])
    p = jnp.concatenate([own[0:1, 0:STARS], own[0:1, 64 : 64 + STARS], own[1:2, 0:STARS]], axis=0)
    cell_out[...] = summed[3:6] - p * summed[6:7]


def correct_kernel(pos, vel, acc, jerk, parts, cell, first, second, pos_out, vel_out, gal_out):
    gal_out[:, 0 : 2 * LEAF] = first[...]
    gal_out[:, 2 * LEAF : 4 * LEAF] = second[...]
    summed = parts[0] + parts[1] + parts[2] + parts[3]
    new_acc = summed[0:3, 0:STARS] + cell[...]
    new_jerk = summed[3:6, 0:STARS]
    new_vel = (
        vel[...]
        + TIME_STEP * 0.5 * (acc[...] + new_acc)
        + STEP_SQ / 12.0 * (jerk[...] - new_jerk)
    )
    vel_out[...] = new_vel
    pos_out[...] = (
        pos[...]
        + TIME_STEP * 0.5 * (vel[...] + new_vel)
        + STEP_SQ / 12.0 * (acc[...] - new_acc)
    )


def shape(*lengths):
    return jax.ShapeDtypeStruct(lengths, F32)


VMEM_SPEC = pl.BlockSpec(memory_space=pltpu.VMEM)
PARAMS = pltpu.CompilerParams(vmem_limit_bytes=32 * 1024 * 1024)


def call(kernel, out_shape, scratch=(), scalars=0, work=0):
    def run(*operands):
        return pl.pallas_call(
            kernel,
            out_shape=out_shape,
            in_specs=[pl.BlockSpec(memory_space=pltpu.SMEM)] * scalars + [VMEM_SPEC] * (len(operands) - scalars),
            out_specs=jax.tree.map(lambda _: VMEM_SPEC, out_shape),
            scratch_shapes=[pltpu.VMEM(lengths, kind) for lengths, kind in scratch],
            compiler_params=PARAMS,
            cost_estimate=pl.CostEstimate(flops=work, bytes_accessed=400_000, transcendentals=work // 40),
        )(*operands)

    return run


def exchange(x, axis):
    return lax.all_to_all(x, axis, split_axis=0, concat_axis=0, tiled=True)


def body(
    star_pos, star_vel, star_mass, star_acc, star_jerk, gal_pos, gal_vel, gal_mass, group_of, let_send, star_leaf
):
    masses = gal_mass.reshape(1, -1)
    star_rows, own, cells, send = call(
        prepare_kernel, (shape(N_NARROW, 8, LANES), shape(8, LANES), shape(8, LANES), shape(N_Z, 8, LANES))
    )(
        star_pos,
        star_vel,
        star_acc,
        star_jerk,
        star_mass.reshape(1, -1),
        gal_pos,
        masses,
        group_of.reshape(1, -1),
        let_send.reshape(1, -1),
    )
    arrived = exchange(send, Z)
    onward = call(onward_kernel, shape(N_XY, 80, LANES))(arrived.reshape(N_Z * 8, LANES))
    stars = exchange(onward, XY)
    stars, star_rows = lax.optimization_barrier((stars, star_rows))
    siblings = exchange(star_rows, NARROW)
    n_targets = N_NARROW * STARS
    leaf_scratch = [((3, 2 * LEAF, LANES), F32), ((32, 2 * LEAF), F32)]
    gal_first, table = call(
        first_pull_kernel,
        (shape(3, 2 * LEAF), shape(2, 8 * BLOCKS, LANES)),
        [((64 * 8, LANES), F32)] + leaf_scratch,
        scalars=1,
        work=30_000_000,
    )(star_leaf, gal_pos, gal_vel, masses, stars)
    later_stars, table = lax.optimization_barrier((stars, table))
    partial = call(
        hermite_kernel,
        shape(N_NARROW, 8, LANES),
        [
            ((2, 16 * 32, LANES), F32),
            ((n_targets, 64), BF16),
            ((3, n_targets, LANES), F32),
            ((32, n_targets), F32),
            ((3, n_targets, LANES), F32),
        ],
        work=80_000_000,
    )(siblings, later_stars)
    shared = exchange(partial, NARROW)
    gal_second, cell_acc = call(
        second_pull_kernel,
        (shape(3, 2 * LEAF), shape(3, STARS)),
        leaf_scratch + [((32, LANES), F32)],
        work=30_000_000,
    )(gal_pos, gal_vel, own, cells, table)
    star_pos_new, star_vel_new, gal_vel_new = call(
        correct_kernel, (shape(3, STARS), shape(3, STARS), shape(3, 4 * LEAF))
    )(star_pos, star_vel, star_acc, star_jerk, shared, cell_acc, gal_first, gal_second)
    return gal_vel_new, star_pos_new, star_vel_new


def solution(mesh):
    torus = Mesh(mesh.devices.reshape(N_Z, N_XY, N_NARROW), ALL)
    cols = P(None, ALL)
    return jax.shard_map(
        body,
        mesh=torus,
        in_specs=(
            cols,
            cols,
            P(ALL),
            cols,
            cols,
            cols,
            cols,
            P(ALL),
            P(ALL),
            P(ALL, None, None),
            P(ALL, None),
        ),
        out_specs=(cols, cols, cols),
        check_vma=False,
    )
```

```python
import jax
import jax.numpy as jnp
from jax import lax
from jax.experimental import pallas as pl
from jax.experimental.pallas import tpu as pltpu
from jax.sharding import Mesh
from jax.sharding import PartitionSpec as P

GROUPS = 32
LEAF = 128
LANES = 128
TIME_STEP = 0.25
SOFT_SQ = 0.05
STEP_SQ = TIME_STEP * TIME_STEP
HIGHEST = lax.Precision.HIGHEST
F32, BF16 = jnp.float32, jnp.bfloat16
LANE_BY_LANE = (((1,), (1,)), ((), ()))

Z, XY, NARROW = "wide_z", "wide_xy", "narrow"
ALL = (Z, XY, NARROW)
N_Z, N_XY, N_NARROW = 16, 8, 4
STARS = 64
STAR_ROWS = 4
PER_BLOCK = 2 * LANES


def predict(pos, vel, acc, jerk):
    pred_pos = pos + TIME_STEP * vel + STEP_SQ * 0.5 * acc + STEP_SQ * TIME_STEP / 6.0 * jerk
    pred_vel = vel + TIME_STEP * acc + STEP_SQ * 0.5 * jerk
    return pred_pos, pred_vel


def prepare_kernel(*refs):
    sources, outs, held, done = refs[:9], refs[9:13], refs[13:22], refs[22]
    own_out, cells_out, send_out, state_out = outs
    copies = [pltpu.make_async_copy(sources[k], held[k], done.at[k]) for k in range(9)]
    for copy in copies:
        copy.start()
    for copy in copies:
        copy.wait()
    pos, vel, acc, jerk, mass, gpos, gmass, group, let = held
    for k, ref in enumerate((pos, vel, acc, jerk)):
        state_out[k] = ref[...]
    pred_pos, pred_vel = predict(pos[...], vel[...], acc[...], jerk[...])
    zero = jnp.zeros((1, STARS), F32)
    rows = [
        (pred_pos[0:1], pred_pos[1:2]),
        (pred_pos[2:3], pred_vel[0:1]),
        (pred_vel[1:2], pred_vel[2:3]),
        (mass[...], zero),
    ]
    packed = jnp.concatenate([jnp.concatenate(pair, axis=1) for pair in rows], axis=0)
    own_out[...] = jnp.concatenate([packed, jnp.zeros((4, LANES), F32)], axis=0)
    leaf_rows = []
    for leaf in range(4):
        span = pl.ds(leaf * LEAF, LEAF)
        m = gmass[:, span]
        stacked = jnp.concatenate([gpos[:, span] * m, m, jnp.zeros((4, LEAF), F32)], axis=0)
        onehot = jnp.where(
            lax.broadcasted_iota(jnp.int32, (GROUPS, LEAF), 0) == group[:, span], 1.0, 0.0
        )
        sums = lax.dot_general(stacked, onehot, LANE_BY_LANE, precision=HIGHEST, preferred_element_type=F32)
        total = sums[3:4]
        centre = sums[0:3] / total
        leaf_rows.append(
            jnp.concatenate([centre[0:1], centre[1:2], centre[2:3], total], axis=1)
        )
    cells_out[...] = jnp.concatenate(leaf_rows + [jnp.zeros((4, LANES), F32)], axis=0)
    ids = let[...].astype(F32)
    lane = lax.broadcasted_iota(jnp.int32, (1, LANES), 1)
    listed = jnp.logical_and(lane >= 64, lane < 64 + N_XY)
    for z in range(N_Z):
        turned = pltpu.roll(ids, (64 - N_XY * z) % LANES, 1)
        last = jnp.where(listed, turned, packed[3:4])
        send_out[z] = jnp.concatenate([packed[0:3], last] + leaf_rows, axis=0)


def onward_kernel(arrived, out):
    flat = arrived
    for pair in range(N_Z // 2):
        both = jnp.concatenate(
            [flat[16 * pair : 16 * pair + 4, :], flat[16 * pair + 8 : 16 * pair + 12, :]], axis=0
        )
        for e in range(N_XY):
            out[e, 8 * pair : 8 * pair + 8, :] = both
    ids = flat[pl.ds(3, N_Z, stride=8), :]
    cells = [flat[pl.ds(4 + leaf, N_Z, stride=8), :] for leaf in range(4)]
    for e in range(N_XY):
        which = jnp.broadcast_to(ids[:, 64 + e : 65 + e], (N_Z, LANES))
        rows = jnp.zeros((N_Z, LANES), F32)
        for leaf in range(4):
            rows = jnp.where(which == float(leaf), cells[leaf], rows)
        out[e, 64:80, :] = rows


def low_lanes(shape):
    return lax.broadcasted_iota(jnp.int32, shape, 1) < 64


def star_plane_pair(stars, r):
    low = low_lanes((N_XY // 2 * N_Z, LANES))
    picked = [stars[e, pl.ds(r, N_Z, stride=STAR_ROWS), :] for e in range(N_XY)]
    first = jnp.concatenate(picked[: N_XY // 2], axis=0)
    second = jnp.concatenate(picked[N_XY // 2 :], axis=0)
    return (
        jnp.where(low, first, pltpu.roll(second, 64, 1)),
        jnp.where(low, pltpu.roll(first, 64, 1), second),
    )


def row_sums(x):
    ones = jnp.ones((8, LANES), F32)
    return lax.dot_general(ones, x, LANE_BY_LANE, precision=HIGHEST, preferred_element_type=F32)[0:1]


def split3(x):
    high = x.astype(BF16).astype(F32)
    rest = x - high
    middle = rest.astype(BF16).astype(F32)
    return high, middle, rest - middle


def source_slots(x):
    h, m, l = split3(x)
    none = jnp.zeros_like(x)
    return jnp.concatenate([h, h, h, m, m, l, none, none], axis=0).astype(BF16)


def target_slots(x):
    h, m, l = split3(x)
    rows = jnp.concatenate([h, m, l, h, m, h] + [jnp.zeros_like(x)] * 10, axis=0)
    return jnp.transpose(rows)[:, 0:64].astype(BF16)


def weighted(source, weight):
    h, m, l = split3(source)
    parts = jnp.concatenate([h, m, l, jnp.zeros_like(source)], axis=0).astype(BF16)
    high = weight.astype(BF16)
    low = (weight - high.astype(F32)).astype(BF16)
    return lax.dot_general(parts, high, LANE_BY_LANE, preferred_element_type=F32) + lax.dot_general(
        parts, low, LANE_BY_LANE, preferred_element_type=F32
    )


def add_parts(x):
    return x[0:8] + x[8:16] + x[16:24]


def twice(x):
    return jnp.concatenate([x, x], axis=1)


def store_rows(ref, stride, row, plane):
    blocks = plane.shape[0] // 2
    ref[0, pl.ds(row, blocks, stride=stride), :] = plane[:blocks]
    ref[1, pl.ds(row, blocks, stride=stride), :] = plane[blocks:]


def load_block(ref, at):
    return jnp.concatenate([ref[half, pl.ds(at, 8), :] for half in range(2)], axis=1)


def hermite_kernel(own, near, middle, far, stars, out, table, slots, here, main, drag):
    n_targets = N_NARROW * STARS
    x, y = star_plane_pair(stars, 0)
    z, u = star_plane_pair(stars, 1)
    v, w = star_plane_pair(stars, 2)
    m, _ = star_plane_pair(stars, 3)
    product = m * (x * u + y * v + z * w)
    for row, plane in enumerate((x, y, z)):
        store_rows(table, 16, row, plane)
    for row, plane in enumerate((m * x, m * y, m * z, m * u, m * v, m * w, m, product)):
        store_rows(table, 16, 8 + row, plane)
    comps = [[] for _ in range(6)]
    for n in range(N_NARROW):
        block = (own, near, middle, far)[n][...]
        for c in range(6):
            comps[c].append(block[c // 2 : c // 2 + 1, 64 * (c % 2) : 64 * (c % 2) + 64])
    rows = [jnp.concatenate(parts, axis=1) for parts in comps]
    p = jnp.concatenate(rows[0:3], axis=0)
    q = jnp.concatenate(rows[3:6], axis=0)
    own_product = jnp.sum(p * q, axis=0, keepdims=True)
    slots[...] = target_slots(
        jnp.concatenate([-q, -p, own_product, jnp.ones((1, n_targets), F32)], axis=0)
    )
    turned = jnp.transpose(jnp.concatenate([p, jnp.zeros((5, n_targets), F32)], axis=0))
    for c in range(3):
        here[c] = jnp.broadcast_to(turned[:, c : c + 1], (n_targets, LANES))
    main[...] = jnp.zeros(main.shape, F32)
    drag[...] = jnp.zeros(drag.shape, F32)

    def block(b, _):
        at = pl.multiple_of(b * 16, 16)
        g = load_block(table, at)
        s = load_block(table, at + 8)
        dx, dy, dz = [g[c : c + 1] - twice(here[c]) for c in range(3)]
        inv = lax.rsqrt(dx * dx + (dy * dy + (dz * dz + SOFT_SQ)))
        approach = jnp.dot(slots[...], source_slots(s), preferred_element_type=F32)
        inv2 = inv * inv
        weight = inv * inv2
        main[...] += weighted(s, weight)
        pulled = weight * inv2 * approach
        for c, d in enumerate((dx, dy, dz)):
            term = pulled * d
            drag[c] += term[:, 0:LANES] + term[:, LANES:PER_BLOCK]
        return 0

    lax.fori_loop(0, table.shape[1] // 16, block, 0, unroll=4)
    total = add_parts(main[...])
    accel = total[0:3] - p * total[6:7]
    dragged = jnp.concatenate([row_sums(drag[c]) for c in range(3)], axis=0)
    jerk = total[3:6] - q * total[6:7] - 3.0 * dragged
    both = jnp.concatenate([accel, jerk, jnp.zeros((2, n_targets), F32)], axis=0)
    me = lax.axis_index(NARROW)
    for n in range(N_NARROW):
        owner = lax.rem(me + (N_NARROW - n), N_NARROW)
        out[owner, :, 0:STARS] = both[:, n * STARS : (n + 1) * STARS]


CELL_BLOCKS = 16
BODY_BLOCK = 16
STAR_BLOCK = 18
BLOCKS = 26


def by_group(picked):
    lane_group = lax.broadcasted_iota(jnp.int32, picked[0].shape, 1) // GROUPS
    out = []
    for c in range(4):
        plane = picked[c]
        for k in range(4):
            if k != c:
                plane = jnp.where(lane_group == k, pltpu.roll(picked[k], (GROUPS * (k - c)) % LANES, 1), plane)
        out.append(plane)
    return out


def table_rows(x, y, z, m):
    return (x, y, z, m * x, m * y, m * z, m)


def build_table(leaf_ref, gpos, gmass, stars, table, splanes):
    quarter = N_XY // 4
    parts = [
        jnp.concatenate([stars[e, 64:80, :] for e in range(quarter * k, quarter * (k + 1))], axis=0)
        for k in range(4)
    ]
    for row, plane in enumerate(table_rows(*by_group(parts))):
        store_rows(table, 8, row, plane)
    for half in range(2):
        spot = slice(8 * (BODY_BLOCK + half), 8 * (BODY_BLOCK + half) + 7)
        for side in range(2):
            span = slice(half * PER_BLOCK + side * LANES, half * PER_BLOCK + (side + 1) * LANES)
            m = gmass[:, span]
            table[side, spot, :] = jnp.concatenate([gpos[:, span], gpos[:, span] * m, m], axis=0)
    x, y = star_plane_pair(stars, 0)
    z, _ = star_plane_pair(stars, 1)
    m, _ = star_plane_pair(stars, 3)
    for c, plane in enumerate((x, y, z, m)):
        splanes[pl.ds(c, 64, stride=8), :] = plane
    low = low_lanes((8, LANES))
    for leaf in range(4):
        for pair in range(4):
            sides = []
            for side in range(2):
                b = leaf_ref[leaf, 2 * pair + side]
                place = (b % N_XY) * N_Z + b // N_XY
                upper = place // 64
                rows = splanes[pl.ds(pl.multiple_of((place - 64 * upper) * 8, 8), 8), :]
                sides.append(jnp.where(upper == side, rows, pltpu.roll(rows, 64, 1)))
            rows = jnp.where(low, sides[0], sides[1])
            m = rows[3:4]
            first = 8 * (STAR_BLOCK + 2 * leaf + pair // 2)
            table[pair % 2, first : first + 7, :] = jnp.concatenate(
                [rows[0:3], rows[0:3] * m, m], axis=0
            )


def pull_of(block, here):
    dx, dy, dz = [block[c : c + 1] - here[c] for c in range(3)]
    inv = lax.rsqrt(dx * dx + (dy * dy + (dz * dz + SOFT_SQ)))
    return weighted(block, inv * (inv * inv))


def pull_kernel(leaf_ref, gpos, gvel, gmass, stars, own, cells, gal_out, cell_out, table, splanes, here, total):
    table[...] = jnp.zeros(table.shape, F32)
    splanes[...] = jnp.zeros(splanes.shape, F32)
    build_table(leaf_ref, gpos, gmass, stars, table, splanes)
    bodies, half = 4 * LEAF, 2 * LEAF
    p = gpos[...]
    turned = jnp.transpose(jnp.concatenate([p, jnp.zeros((5, bodies), F32)], axis=0))
    for c in range(3):
        here[c] = jnp.broadcast_to(turned[:, c : c + 1], (bodies, LANES))
    total[...] = jnp.zeros(total.shape, F32)

    def block(b, _):
        g = load_block(table, pl.multiple_of(b * 8, 8))
        for first in (0, half):
            spot = slice(first, first + half)
            total[:, spot] += pull_of(g, [twice(here[c, spot]) for c in range(3)])
        return 0

    lax.fori_loop(0, STAR_BLOCK, block, 0, unroll=2)
    for leaf in range(4):
        spot = slice(leaf * LEAF, (leaf + 1) * LEAF)
        for k in range(2):
            g = load_block(table, 8 * (STAR_BLOCK + 2 * leaf + k))
            total[:, spot] += pull_of(g, [twice(here[c, spot]) for c in range(3)])
    summed = add_parts(total[...])
    gal_out[...] = gvel[...] + TIME_STEP * (summed[3:6] - p * summed[6:7])

    turned = jnp.transpose(own[...])
    at = [
        jnp.broadcast_to(turned[64 * (c % 2) : 64 * (c % 2) + 64, c // 2 : c // 2 + 1], (STARS, LANES))
        for c in range(3)
    ]

    def add_pull(source, sums):
        dx, dy, dz = [source[c] - at[c] for c in range(3)]
        inv = lax.rsqrt(dx * dx + (dy * dy + (dz * dz + SOFT_SQ)))
        weight = source[3] * inv * (inv * inv)
        return sums[0] + weight * dx, sums[1] + weight * dy, sums[2] + weight * dz

    def row(b, sums):
        for side in range(2):
            sums = add_pull([table[side, pl.ds(b * 8 + r, 1), :] for r in (0, 1, 2, 6)], sums)
        return sums

    zero = jnp.zeros((STARS, LANES), F32)
    res = add_pull(by_group([cells[k : k + 1] for k in range(4)]), (zero,) * 3)
    res = lax.fori_loop(0, CELL_BLOCKS, row, res, unroll=2)
    for c in range(3):
        cell_out[c : c + 1] = row_sums(res[c])


def correct_kernel(state, parts, cell, pos_out, vel_out):
    pos, vel, acc, jerk = [state[k] for k in range(4)]
    summed = parts[0] + parts[1] + parts[2] + parts[3]
    new_acc = summed[0:3, 0:STARS] + cell[...]
    new_jerk = summed[3:6, 0:STARS]
    new_vel = (
        vel
        + TIME_STEP * 0.5 * (acc + new_acc)
        + STEP_SQ / 12.0 * (jerk - new_jerk)
    )
    vel_out[...] = new_vel
    pos_out[...] = (
        pos
        + TIME_STEP * 0.5 * (vel + new_vel)
        + STEP_SQ / 12.0 * (acc - new_acc)
    )


def shape(*lengths):
    return jax.ShapeDtypeStruct(lengths, F32)


VMEM_SPEC = pl.BlockSpec(memory_space=pltpu.VMEM)


def call(kernel, out_shape, scratch=(), scalars=0, work=0, space=VMEM_SPEC, extra=(), limit=32 * 1024 * 1024):
    def run(*operands):
        return pl.pallas_call(
            kernel,
            out_shape=out_shape,
            in_specs=[pl.BlockSpec(memory_space=pltpu.SMEM)] * scalars + [space] * (len(operands) - scalars),
            out_specs=jax.tree.map(lambda _: VMEM_SPEC, out_shape),
            scratch_shapes=[pltpu.VMEM(lengths, kind) for lengths, kind in scratch] + list(extra),
            compiler_params=pltpu.CompilerParams(vmem_limit_bytes=limit),
            cost_estimate=pl.CostEstimate(flops=work, bytes_accessed=400_000, transcendentals=work // 40),
        )(*operands)

    return run


def exchange(x, axis):
    return lax.all_to_all(x, axis, split_axis=0, concat_axis=0, tiled=True)


def body(
    star_pos, star_vel, star_mass, star_acc, star_jerk, gal_pos, gal_vel, gal_mass, group_of, let_send, star_leaf
):
    masses = gal_mass.reshape(1, -1)
    operands = (
        star_pos,
        star_vel,
        star_acc,
        star_jerk,
        star_mass.reshape(1, -1),
        gal_pos,
        masses,
        group_of.reshape(1, -1),
        let_send.reshape(1, -1),
    )
    own, cells, send, state = call(
        prepare_kernel,
        (shape(8, LANES), shape(8, LANES), shape(N_Z, 8, LANES), shape(4, 3, STARS)),
        [(x.shape, x.dtype) for x in operands],
        space=pl.BlockSpec(memory_space=pltpu.HBM),
        extra=[pltpu.SemaphoreType.DMA((len(operands),))],
        limit=None,
    )(*operands)
    arrived = exchange(send, Z)
    onward = call(onward_kernel, shape(N_XY, 80, LANES))(arrived.reshape(N_Z * 8, LANES))
    stars = exchange(onward, XY)
    siblings = [
        lax.ppermute(own, NARROW, [(n, (n + k) % N_NARROW) for n in range(N_NARROW)])
        for k in range(1, N_NARROW)
    ]
    n_targets = N_NARROW * STARS
    partial = call(
        hermite_kernel,
        shape(N_NARROW, 8, LANES),
        [
            ((2, 16 * 32, LANES), F32),
            ((n_targets, 64), BF16),
            ((3, n_targets, LANES), F32),
            ((32, n_targets), F32),
            ((3, n_targets, LANES), F32),
        ],
        work=80_000_000,
    )(own, *siblings, stars)
    shared = exchange(partial, NARROW)
    gal_vel_new, cell_acc = call(
        pull_kernel,
        (shape(3, 4 * LEAF), shape(3, STARS)),
        [
            ((2, 8 * BLOCKS, LANES), F32),
            ((64 * 8, LANES), F32),
            ((3, 4 * LEAF, LANES), F32),
            ((32, 4 * LEAF), F32),
        ],
        scalars=1,
        work=60_000_000,
    )(star_leaf, gal_pos, gal_vel, masses, stars, own, cells)
    star_pos_new, star_vel_new = call(correct_kernel, (shape(3, STARS), shape(3, STARS)))(
        state, shared, cell_acc
    )
    return gal_vel_new, star_pos_new, star_vel_new


def solution(mesh):
    torus = Mesh(mesh.devices.reshape(N_Z, N_XY, N_NARROW), ALL)
    cols = P(None, ALL)
    return jax.shard_map(
        body,
        mesh=torus,
        in_specs=(
            cols,
            cols,
            P(ALL),
            cols,
            cols,
            cols,
            cols,
            P(ALL),
            P(ALL),
            P(ALL, None, None),
            P(ALL, None),
        ),
        out_specs=(cols, cols, cols),
        check_vma=False,
    )
```

```python
import jax
import jax.numpy as jnp
from jax import lax
from jax.experimental import pallas as pl
from jax.experimental.pallas import tpu as pltpu
from jax.sharding import Mesh
from jax.sharding import PartitionSpec as P

GROUPS = 32
LEAF = 128
LANES = 128
TIME_STEP = 0.25
SOFT_SQ = 0.05
STEP_SQ = TIME_STEP * TIME_STEP
HIGHEST = lax.Precision.HIGHEST
F32, BF16 = jnp.float32, jnp.bfloat16
LANE_BY_LANE = (((1,), (1,)), ((), ()))

Z, XY, NARROW = "wide_z", "wide_xy", "narrow"
ALL = (Z, XY, NARROW)
N_Z, N_XY, N_NARROW = 16, 8, 4
STARS = 64
STAR_ROWS = 4
PER_BLOCK = 2 * LANES


def predict(pos, vel, acc, jerk):
    pred_pos = pos + TIME_STEP * vel + STEP_SQ * 0.5 * acc + STEP_SQ * TIME_STEP / 6.0 * jerk
    pred_vel = vel + TIME_STEP * acc + STEP_SQ * 0.5 * jerk
    return pred_pos, pred_vel


def prepare_kernel(*refs):
    sources, outs, held, done = refs[:9], refs[9:13], refs[13:22], refs[22]
    own_out, cells_out, send_out, state_out = outs
    copies = [pltpu.make_async_copy(sources[k], held[k], done.at[k]) for k in range(9)]
    for copy in copies:
        copy.start()
    for copy in copies:
        copy.wait()
    pos, vel, acc, jerk, mass, gpos, gmass, group, let = held
    for k, ref in enumerate((pos, vel, acc, jerk)):
        state_out[k] = ref[...]
    pred_pos, pred_vel = predict(pos[...], vel[...], acc[...], jerk[...])
    zero = jnp.zeros((1, STARS), F32)
    rows = [
        (pred_pos[0:1], pred_pos[1:2]),
        (pred_pos[2:3], pred_vel[0:1]),
        (pred_vel[1:2], pred_vel[2:3]),
        (mass[...], zero),
    ]
    packed = jnp.concatenate([jnp.concatenate(pair, axis=1) for pair in rows], axis=0)
    own_out[...] = jnp.concatenate([packed, jnp.zeros((4, LANES), F32)], axis=0)
    leaf_rows = []
    for leaf in range(4):
        span = pl.ds(leaf * LEAF, LEAF)
        m = gmass[:, span]
        stacked = jnp.concatenate([gpos[:, span] * m, m, jnp.zeros((4, LEAF), F32)], axis=0)
        onehot = jnp.where(
            lax.broadcasted_iota(jnp.int32, (GROUPS, LEAF), 0) == group[:, span], 1.0, 0.0
        )
        sums = lax.dot_general(stacked, onehot, LANE_BY_LANE, precision=HIGHEST, preferred_element_type=F32)
        total = sums[3:4]
        centre = sums[0:3] / total
        leaf_rows.append(
            jnp.concatenate([centre[0:1], centre[1:2], centre[2:3], total], axis=1)
        )
    cells_out[...] = jnp.concatenate(leaf_rows + [jnp.zeros((4, LANES), F32)], axis=0)
    ids = let[...].astype(F32)
    lane = lax.broadcasted_iota(jnp.int32, (1, LANES), 1)
    listed = jnp.logical_and(lane >= 64, lane < 64 + N_XY)
    for z in range(N_Z):
        turned = pltpu.roll(ids, (64 - N_XY * z) % LANES, 1)
        last = jnp.where(listed, turned, packed[3:4])
        send_out[z] = jnp.concatenate([packed[0:3], last] + leaf_rows, axis=0)


def onward_kernel(arrived, out):
    flat = arrived
    for pair in range(N_Z // 2):
        both = jnp.concatenate(
            [flat[16 * pair : 16 * pair + 4, :], flat[16 * pair + 8 : 16 * pair + 12, :]], axis=0
        )
        for e in range(N_XY):
            out[e, 8 * pair : 8 * pair + 8, :] = both
    ids = flat[pl.ds(3, N_Z, stride=8), :]
    cells = [flat[pl.ds(4 + leaf, N_Z, stride=8), :] for leaf in range(4)]
    for e in range(N_XY):
        which = jnp.broadcast_to(ids[:, 64 + e : 65 + e], (N_Z, LANES))
        rows = jnp.zeros((N_Z, LANES), F32)
        for leaf in range(4):
            rows = jnp.where(which == float(leaf), cells[leaf], rows)
        out[e, 64:80, :] = rows


def low_lanes(shape):
    return lax.broadcasted_iota(jnp.int32, shape, 1) < 64


def star_plane_pair(stars, r):
    low = low_lanes((N_XY // 2 * N_Z, LANES))
    picked = [stars[e, pl.ds(r, N_Z, stride=STAR_ROWS), :] for e in range(N_XY)]
    first = jnp.concatenate(picked[: N_XY // 2], axis=0)
    second = jnp.concatenate(picked[N_XY // 2 :], axis=0)
    return (
        jnp.where(low, first, pltpu.roll(second, 64, 1)),
        jnp.where(low, pltpu.roll(first, 64, 1), second),
    )


def row_sums(x):
    ones = jnp.ones((8, LANES), F32)
    return lax.dot_general(ones, x, LANE_BY_LANE, precision=HIGHEST, preferred_element_type=F32)[0:1]


def split3(x):
    high = x.astype(BF16).astype(F32)
    rest = x - high
    middle = rest.astype(BF16).astype(F32)
    return high, middle, rest - middle


def source_slots(x):
    h, m, l = split3(x)
    none = jnp.zeros_like(x)
    return jnp.concatenate([h, h, h, m, m, l, none, none], axis=0).astype(BF16)


def target_slots(x):
    h, m, l = split3(x)
    rows = jnp.concatenate([h, m, l, h, m, h] + [jnp.zeros_like(x)] * 10, axis=0)
    return jnp.transpose(rows)[:, 0:64].astype(BF16)


def weighted(source, weight):
    h, m, l = split3(source)
    parts = jnp.concatenate([h, m, l, jnp.zeros_like(source)], axis=0).astype(BF16)
    high = weight.astype(BF16)
    low = (weight - high.astype(F32)).astype(BF16)
    return lax.dot_general(parts, high, LANE_BY_LANE, preferred_element_type=F32) + lax.dot_general(
        parts, low, LANE_BY_LANE, preferred_element_type=F32
    )


def add_parts(x):
    return x[0:8] + x[8:16] + x[16:24]


def twice(x):
    return jnp.concatenate([x, x], axis=1)


def store_rows(ref, stride, row, plane):
    blocks = plane.shape[0] // 2
    ref[0, pl.ds(row, blocks, stride=stride), :] = plane[:blocks]
    ref[1, pl.ds(row, blocks, stride=stride), :] = plane[blocks:]


def load_block(ref, at):
    return jnp.concatenate([ref[half, pl.ds(at, 8), :] for half in range(2)], axis=1)


def hermite_kernel(own, near, middle, far, stars, out, table, slots, here, main, drag):
    n_targets = N_NARROW * STARS
    x, y = star_plane_pair(stars, 0)
    z, u = star_plane_pair(stars, 1)
    v, w = star_plane_pair(stars, 2)
    m, _ = star_plane_pair(stars, 3)
    product = m * (x * u + y * v + z * w)
    for row, plane in enumerate((x, y, z)):
        store_rows(table, 16, row, plane)
    for row, plane in enumerate((m * x, m * y, m * z, m * u, m * v, m * w, m, product)):
        store_rows(table, 16, 8 + row, plane)
    comps = [[] for _ in range(6)]
    for n in range(N_NARROW):
        block = (own, near, middle, far)[n][...]
        for c in range(6):
            comps[c].append(block[c // 2 : c // 2 + 1, 64 * (c % 2) : 64 * (c % 2) + 64])
    rows = [jnp.concatenate(parts, axis=1) for parts in comps]
    p = jnp.concatenate(rows[0:3], axis=0)
    q = jnp.concatenate(rows[3:6], axis=0)
    own_product = jnp.sum(p * q, axis=0, keepdims=True)
    slots[...] = target_slots(
        jnp.concatenate([-q, -p, own_product, jnp.ones((1, n_targets), F32)], axis=0)
    )
    turned = jnp.transpose(jnp.concatenate([p, jnp.zeros((5, n_targets), F32)], axis=0))
    for c in range(3):
        here[c] = jnp.broadcast_to(turned[:, c : c + 1], (n_targets, LANES))
    main[...] = jnp.zeros(main.shape, F32)
    drag[...] = jnp.zeros(drag.shape, F32)

    def block(b, _):
        at = pl.multiple_of(b * 16, 16)
        g = load_block(table, at)
        s = load_block(table, at + 8)
        dx, dy, dz = [g[c : c + 1] - twice(here[c]) for c in range(3)]
        inv = lax.rsqrt(dx * dx + (dy * dy + (dz * dz + SOFT_SQ)))
        approach = jnp.dot(slots[...], source_slots(s), preferred_element_type=F32)
        inv2 = inv * inv
        weight = inv * inv2
        main[...] += weighted(s, weight)
        pulled = weight * inv2 * approach
        for c, d in enumerate((dx, dy, dz)):
            term = pulled * d
            drag[c] += term[:, 0:LANES] + term[:, LANES:PER_BLOCK]
        return 0

    lax.fori_loop(0, table.shape[1] // 16, block, 0, unroll=4)
    total = add_parts(main[...])
    accel = total[0:3] - p * total[6:7]
    dragged = jnp.concatenate([row_sums(drag[c]) for c in range(3)], axis=0)
    jerk = total[3:6] - q * total[6:7] - 3.0 * dragged
    both = jnp.concatenate([accel, jerk, jnp.zeros((2, n_targets), F32)], axis=0)
    me = lax.axis_index(NARROW)
    for n in range(N_NARROW):
        owner = lax.rem(me + (N_NARROW - n), N_NARROW)
        out[owner, :, 0:STARS] = both[:, n * STARS : (n + 1) * STARS]


CELL_BLOCKS = 16
BODY_BLOCK = 16
STAR_BLOCK = 18
BLOCKS = 26


def by_group(picked):
    lane_group = lax.broadcasted_iota(jnp.int32, picked[0].shape, 1) // GROUPS
    out = []
    for c in range(4):
        plane = picked[c]
        for k in range(4):
            if k != c:
                plane = jnp.where(lane_group == k, pltpu.roll(picked[k], (GROUPS * (k - c)) % LANES, 1), plane)
        out.append(plane)
    return out


def table_rows(x, y, z, m):
    return (x, y, z, m * x, m * y, m * z, m)


def build_table(leaf_ref, gpos, gmass, stars, table, splanes):
    quarter = N_XY // 4
    parts = [
        jnp.concatenate([stars[e, 64:80, :] for e in range(quarter * k, quarter * (k + 1))], axis=0)
        for k in range(4)
    ]
    for row, plane in enumerate(table_rows(*by_group(parts))):
        store_rows(table, 8, row, plane)
    for half in range(2):
        spot = slice(8 * (BODY_BLOCK + half), 8 * (BODY_BLOCK + half) + 7)
        for side in range(2):
            span = slice(half * PER_BLOCK + side * LANES, half * PER_BLOCK + (side + 1) * LANES)
            m = gmass[:, span]
            table[side, spot, :] = jnp.concatenate([gpos[:, span], gpos[:, span] * m, m], axis=0)
    x, y = star_plane_pair(stars, 0)
    z, _ = star_plane_pair(stars, 1)
    m, _ = star_plane_pair(stars, 3)
    for c, plane in enumerate((x, y, z, m)):
        splanes[pl.ds(c, 64, stride=8), :] = plane
    low = low_lanes((8, LANES))
    for leaf in range(4):
        for pair in range(4):
            sides = []
            for side in range(2):
                b = leaf_ref[leaf, 2 * pair + side]
                place = (b % N_XY) * N_Z + b // N_XY
                upper = place // 64
                rows = splanes[pl.ds(pl.multiple_of((place - 64 * upper) * 8, 8), 8), :]
                sides.append(jnp.where(upper == side, rows, pltpu.roll(rows, 64, 1)))
            rows = jnp.where(low, sides[0], sides[1])
            m = rows[3:4]
            first = 8 * (STAR_BLOCK + 2 * leaf + pair // 2)
            table[pair % 2, first : first + 7, :] = jnp.concatenate(
                [rows[0:3], rows[0:3] * m, m], axis=0
            )


def pull_of(block, here):
    dx, dy, dz = [block[c : c + 1] - here[c] for c in range(3)]
    inv = lax.rsqrt(dx * dx + (dy * dy + (dz * dz + SOFT_SQ)))
    return weighted(block, inv * (inv * inv))


def pull_kernel(leaf_ref, gpos, gvel, gmass, stars, own, cells, gal_out, cell_out, table, splanes, here, total):
    table[...] = jnp.zeros(table.shape, F32)
    splanes[...] = jnp.zeros(splanes.shape, F32)
    build_table(leaf_ref, gpos, gmass, stars, table, splanes)
    bodies, half = 4 * LEAF, 2 * LEAF
    p = gpos[...]
    turned = jnp.transpose(jnp.concatenate([p, jnp.zeros((5, bodies), F32)], axis=0))
    for c in range(3):
        here[c] = jnp.broadcast_to(turned[:, c : c + 1], (bodies, LANES))
    total[...] = jnp.zeros(total.shape, F32)

    def block(b, _):
        g = load_block(table, pl.multiple_of(b * 8, 8))
        for first in (0, half):
            spot = slice(first, first + half)
            total[:, spot] += pull_of(g, [twice(here[c, spot]) for c in range(3)])
        return 0

    lax.fori_loop(0, STAR_BLOCK, block, 0, unroll=2)
    for leaf in range(4):
        spot = slice(leaf * LEAF, (leaf + 1) * LEAF)
        for k in range(2):
            g = load_block(table, 8 * (STAR_BLOCK + 2 * leaf + k))
            total[:, spot] += pull_of(g, [twice(here[c, spot]) for c in range(3)])
    summed = add_parts(total[...])
    gal_out[...] = gvel[...] + TIME_STEP * (summed[3:6] - p * summed[6:7])

    turned = jnp.transpose(own[...])
    at = [
        jnp.broadcast_to(turned[64 * (c % 2) : 64 * (c % 2) + 64, c // 2 : c // 2 + 1], (STARS, LANES))
        for c in range(3)
    ]

    def add_pull(source, sums):
        dx, dy, dz = [source[c] - at[c] for c in range(3)]
        inv = lax.rsqrt(dx * dx + (dy * dy + (dz * dz + SOFT_SQ)))
        weight = source[3] * inv * (inv * inv)
        return sums[0] + weight * dx, sums[1] + weight * dy, sums[2] + weight * dz

    def row(b, sums):
        for side in range(2):
            sums = add_pull([table[side, pl.ds(b * 8 + r, 1), :] for r in (0, 1, 2, 6)], sums)
        return sums

    zero = jnp.zeros((STARS, LANES), F32)
    res = add_pull(by_group([cells[k : k + 1] for k in range(4)]), (zero,) * 3)
    res = lax.fori_loop(0, CELL_BLOCKS, row, res, unroll=2)
    for c in range(3):
        cell_out[c : c + 1] = row_sums(res[c])


def correct_kernel(state, parts, cell, pos_out, vel_out):
    pos, vel, acc, jerk = [state[k] for k in range(4)]
    summed = parts[0] + parts[1] + parts[2] + parts[3]
    new_acc = summed[0:3, 0:STARS] + cell[...]
    new_jerk = summed[3:6, 0:STARS]
    new_vel = (
        vel
        + TIME_STEP * 0.5 * (acc + new_acc)
        + STEP_SQ / 12.0 * (jerk - new_jerk)
    )
    vel_out[...] = new_vel
    pos_out[...] = (
        pos
        + TIME_STEP * 0.5 * (vel + new_vel)
        + STEP_SQ / 12.0 * (acc - new_acc)
    )


def shape(*lengths):
    return jax.ShapeDtypeStruct(lengths, F32)


VMEM_SPEC = pl.BlockSpec(memory_space=pltpu.VMEM)


def call(kernel, out_shape, scratch=(), scalars=0, work=0, space=VMEM_SPEC, extra=(), limit=32 * 1024 * 1024):
    def run(*operands):
        return pl.pallas_call(
            kernel,
            out_shape=out_shape,
            in_specs=[pl.BlockSpec(memory_space=pltpu.SMEM)] * scalars + [space] * (len(operands) - scalars),
            out_specs=jax.tree.map(lambda _: VMEM_SPEC, out_shape),
            scratch_shapes=[pltpu.VMEM(lengths, kind) for lengths, kind in scratch] + list(extra),
            compiler_params=pltpu.CompilerParams(vmem_limit_bytes=limit),
            cost_estimate=pl.CostEstimate(flops=work, bytes_accessed=400_000, transcendentals=work // 40),
        )(*operands)

    return run


def exchange(x, axis):
    return lax.all_to_all(x, axis, split_axis=0, concat_axis=0, tiled=True)


def body(
    star_pos, star_vel, star_mass, star_acc, star_jerk, gal_pos, gal_vel, gal_mass, group_of, let_send, star_leaf
):
    masses = gal_mass.reshape(1, -1)
    operands = (
        star_pos,
        star_vel,
        star_acc,
        star_jerk,
        star_mass.reshape(1, -1),
        gal_pos,
        masses,
        group_of.reshape(1, -1),
        let_send.reshape(1, -1),
    )
    own, cells, send, state = call(
        prepare_kernel,
        (shape(8, LANES), shape(8, LANES), shape(N_Z, 8, LANES), shape(4, 3, STARS)),
        [(x.shape, x.dtype) for x in operands],
        space=pl.BlockSpec(memory_space=pltpu.HBM),
        extra=[pltpu.SemaphoreType.DMA((len(operands),))],
        limit=None,
    )(*operands)
    arrived = exchange(send, Z)
    siblings = [
        lax.ppermute(own, NARROW, [(n, (n + k) % N_NARROW) for n in range(N_NARROW)])
        for k in range(1, N_NARROW)
    ]
    arrived, *siblings = lax.optimization_barrier((arrived, *siblings))
    onward = call(onward_kernel, shape(N_XY, 80, LANES))(arrived.reshape(N_Z * 8, LANES))
    stars = exchange(onward, XY)
    n_targets = N_NARROW * STARS
    partial = call(
        hermite_kernel,
        shape(N_NARROW, 8, LANES),
        [
            ((2, 16 * 32, LANES), F32),
            ((n_targets, 64), BF16),
            ((3, n_targets, LANES), F32),
            ((32, n_targets), F32),
            ((3, n_targets, LANES), F32),
        ],
        work=80_000_000,
    )(own, *siblings, stars)
    shared = exchange(partial, NARROW)
    gal_vel_new, cell_acc = call(
        pull_kernel,
        (shape(3, 4 * LEAF), shape(3, STARS)),
        [
            ((2, 8 * BLOCKS, LANES), F32),
            ((64 * 8, LANES), F32),
            ((3, 4 * LEAF, LANES), F32),
            ((32, 4 * LEAF), F32),
        ],
        scalars=1,
        work=60_000_000,
    )(star_leaf, gal_pos, gal_vel, masses, stars, own, cells)
    star_pos_new, star_vel_new = call(correct_kernel, (shape(3, STARS), shape(3, STARS)))(
        state, shared, cell_acc
    )
    return gal_vel_new, star_pos_new, star_vel_new


def solution(mesh):
    torus = Mesh(mesh.devices.reshape(N_Z, N_XY, N_NARROW), ALL)
    cols = P(None, ALL)
    return jax.shard_map(
        body,
        mesh=torus,
        in_specs=(
            cols,
            cols,
            P(ALL),
            cols,
            cols,
            cols,
            cols,
            P(ALL),
            P(ALL),
            P(ALL, None, None),
            P(ALL, None),
        ),
        out_specs=(cols, cols, cols),
        check_vma=False,
    )
```

```python
import jax
import jax.numpy as jnp
from jax import lax
from jax.experimental import pallas as pl
from jax.experimental.pallas import tpu as pltpu
from jax.sharding import Mesh
from jax.sharding import PartitionSpec as P

GROUPS = 32
LEAF = 128
LANES = 128
TIME_STEP = 0.25
SOFT_SQ = 0.05
STEP_SQ = TIME_STEP * TIME_STEP
HIGHEST = lax.Precision.HIGHEST
F32, BF16 = jnp.float32, jnp.bfloat16
LANE_BY_LANE = (((1,), (1,)), ((), ()))

Z, XY, NARROW = "wide_z", "wide_xy", "narrow"
ALL = (Z, XY, NARROW)
N_Z, N_XY, N_NARROW = 16, 8, 4
STARS = 64
STAR_ROWS = 4
PER_BLOCK = 2 * LANES
CHUNK_BLOCKS = N_Z * STARS // PER_BLOCK


def predict(pos, vel, acc, jerk):
    pred_pos = pos + TIME_STEP * vel + STEP_SQ * 0.5 * acc + STEP_SQ * TIME_STEP / 6.0 * jerk
    pred_vel = vel + TIME_STEP * acc + STEP_SQ * 0.5 * jerk
    return pred_pos, pred_vel


def prepare_kernel(*refs):
    sources, outs, held, done = refs[:9], refs[9:13], refs[13:22], refs[22]
    own_out, cells_out, send_out, state_out = outs
    copies = [pltpu.make_async_copy(sources[k], held[k], done.at[k]) for k in range(9)]
    for copy in copies:
        copy.start()
    for copy in copies:
        copy.wait()
    pos, vel, acc, jerk, mass, gpos, gmass, group, let = held
    for k, ref in enumerate((pos, vel, acc, jerk)):
        state_out[k] = ref[...]
    pred_pos, pred_vel = predict(pos[...], vel[...], acc[...], jerk[...])
    zero = jnp.zeros((1, STARS), F32)
    rows = [
        (pred_pos[0:1], pred_pos[1:2]),
        (pred_pos[2:3], pred_vel[0:1]),
        (pred_vel[1:2], pred_vel[2:3]),
        (mass[...], zero),
    ]
    packed = jnp.concatenate([jnp.concatenate(pair, axis=1) for pair in rows], axis=0)
    own_out[...] = jnp.concatenate([packed, jnp.zeros((4, LANES), F32)], axis=0)
    leaf_rows = []
    for leaf in range(4):
        span = pl.ds(leaf * LEAF, LEAF)
        m = gmass[:, span]
        stacked = jnp.concatenate([gpos[:, span] * m, m, jnp.zeros((4, LEAF), F32)], axis=0)
        onehot = jnp.where(
            lax.broadcasted_iota(jnp.int32, (GROUPS, LEAF), 0) == group[:, span], 1.0, 0.0
        )
        sums = lax.dot_general(stacked, onehot, LANE_BY_LANE, precision=HIGHEST, preferred_element_type=F32)
        total = sums[3:4]
        centre = sums[0:3] / total
        leaf_rows.append(
            jnp.concatenate([centre[0:1], centre[1:2], centre[2:3], total], axis=1)
        )
    cells_out[...] = jnp.concatenate(leaf_rows + [jnp.zeros((4, LANES), F32)], axis=0)
    ids = let[...].astype(F32)
    lane = lax.broadcasted_iota(jnp.int32, (1, LANES), 1)
    listed = jnp.logical_and(lane >= 64, lane < 64 + N_XY)
    for z in range(N_Z):
        turned = pltpu.roll(ids, (64 - N_XY * z) % LANES, 1)
        last = jnp.where(listed, turned, packed[3:4])
        send_out[z] = jnp.concatenate([packed[0:3], last] + leaf_rows, axis=0)


def onward_kernel(arrived, out, mine):
    flat = arrived
    for pair in range(N_Z // 2):
        both = jnp.concatenate(
            [flat[16 * pair : 16 * pair + 4, :], flat[16 * pair + 8 : 16 * pair + 12, :]], axis=0
        )
        for e in range(N_XY):
            out[e, 8 * pair : 8 * pair + 8, :] = both
    ids = flat[pl.ds(3, N_Z, stride=8), :]
    cells = [flat[pl.ds(4 + leaf, N_Z, stride=8), :] for leaf in range(4)]
    for e in range(N_XY):
        which = jnp.broadcast_to(ids[:, 64 + e : 65 + e], (N_Z, LANES))
        rows = jnp.zeros((N_Z, LANES), F32)
        for leaf in range(4):
            rows = jnp.where(which == float(leaf), cells[leaf], rows)
        out[e, 64:80, :] = rows
    mine[...] = out[lax.axis_index(XY)]


def low_lanes(shape):
    return lax.broadcasted_iota(jnp.int32, shape, 1) < 64


def star_plane_pair(chunks, r):
    picked = [chunk[pl.ds(r, N_Z, stride=STAR_ROWS), :] for chunk in chunks]
    first = jnp.concatenate([rows[: N_Z // 2] for rows in picked], axis=0)
    second = jnp.concatenate([rows[N_Z // 2 :] for rows in picked], axis=0)
    low = low_lanes(first.shape)
    return (
        jnp.where(low, first, pltpu.roll(second, 64, 1)),
        jnp.where(low, pltpu.roll(first, 64, 1), second),
    )


def other_chunks(stars):
    me = lax.axis_index(XY)
    return [stars.at[lax.rem(me + k, N_XY)] for k in range(1, N_XY)]


def row_sums(x):
    ones = jnp.ones((8, LANES), F32)
    return lax.dot_general(ones, x, LANE_BY_LANE, precision=HIGHEST, preferred_element_type=F32)[0:1]


def split3(x):
    high = x.astype(BF16).astype(F32)
    rest = x - high
    middle = rest.astype(BF16).astype(F32)
    return high, middle, rest - middle


def source_slots(x):
    h, m, l = split3(x)
    none = jnp.zeros_like(x)
    return jnp.concatenate([h, h, h, m, m, l, none, none], axis=0).astype(BF16)


def target_slots(x):
    h, m, l = split3(x)
    rows = jnp.concatenate([h, m, l, h, m, h] + [jnp.zeros_like(x)] * 10, axis=0)
    return jnp.transpose(rows)[:, 0:64].astype(BF16)


def weighted(source, weight):
    h, m, l = split3(source)
    parts = jnp.concatenate([h, m, l, jnp.zeros_like(source)], axis=0).astype(BF16)
    high = weight.astype(BF16)
    low = (weight - high.astype(F32)).astype(BF16)
    return lax.dot_general(parts, high, LANE_BY_LANE, preferred_element_type=F32) + lax.dot_general(
        parts, low, LANE_BY_LANE, preferred_element_type=F32
    )


def add_parts(x):
    return x[0:8] + x[8:16] + x[16:24]


def twice(x):
    return jnp.concatenate([x, x], axis=1)


def store_rows(ref, stride, row, plane):
    blocks = plane.shape[0] // 2
    ref[0, pl.ds(row, blocks, stride=stride), :] = plane[:blocks]
    ref[1, pl.ds(row, blocks, stride=stride), :] = plane[blocks:]


def load_block(ref, at):
    return jnp.concatenate([ref[half, pl.ds(at, 8), :] for half in range(2)], axis=1)


def hermite_partial(own, beside, across, chunks, table, slots, here, main, drag):
    n_targets = N_NARROW * STARS
    x, y = star_plane_pair(chunks, 0)
    z, u = star_plane_pair(chunks, 1)
    v, w = star_plane_pair(chunks, 2)
    m, _ = star_plane_pair(chunks, 3)
    product = m * (x * u + y * v + z * w)
    for row, plane in enumerate((x, y, z)):
        store_rows(table, 16, row, plane)
    for row, plane in enumerate((m * x, m * y, m * z, m * u, m * v, m * w, m, product)):
        store_rows(table, 16, 8 + row, plane)
    comps = [[] for _ in range(6)]
    for n in range(N_NARROW):
        block = (own[...], beside[...], across[0:8], across[8:16])[n]
        for c in range(6):
            comps[c].append(block[c // 2 : c // 2 + 1, 64 * (c % 2) : 64 * (c % 2) + 64])
    rows = [jnp.concatenate(parts, axis=1) for parts in comps]
    p = jnp.concatenate(rows[0:3], axis=0)
    q = jnp.concatenate(rows[3:6], axis=0)
    own_product = jnp.sum(p * q, axis=0, keepdims=True)
    slots[...] = target_slots(
        jnp.concatenate([-q, -p, own_product, jnp.ones((1, n_targets), F32)], axis=0)
    )
    turned = jnp.transpose(jnp.concatenate([p, jnp.zeros((5, n_targets), F32)], axis=0))
    for c in range(3):
        here[c] = jnp.broadcast_to(turned[:, c : c + 1], (n_targets, LANES))
    main[...] = jnp.zeros(main.shape, F32)
    drag[...] = jnp.zeros(drag.shape, F32)

    def block(b, _):
        at = pl.multiple_of(b * 16, 16)
        g = load_block(table, at)
        s = load_block(table, at + 8)
        dx, dy, dz = [g[c : c + 1] - twice(here[c]) for c in range(3)]
        inv = lax.rsqrt(dx * dx + (dy * dy + (dz * dz + SOFT_SQ)))
        approach = jnp.dot(slots[...], source_slots(s), preferred_element_type=F32)
        inv2 = inv * inv
        weight = inv * inv2
        main[...] += weighted(s, weight)
        pulled = weight * inv2 * approach
        for c, d in enumerate((dx, dy, dz)):
            term = pulled * d
            drag[c] += term[:, 0:LANES] + term[:, LANES:PER_BLOCK]
        return 0

    lax.fori_loop(0, CHUNK_BLOCKS * len(chunks), block, 0, unroll=4)
    total = add_parts(main[...])
    accel = total[0:3] - p * total[6:7]
    dragged = jnp.concatenate([row_sums(drag[c]) for c in range(3)], axis=0)
    jerk = total[3:6] - q * total[6:7] - 3.0 * dragged
    both = jnp.concatenate([accel, jerk, jnp.zeros((2, n_targets), F32)], axis=0)
    return both


def early_hermite_kernel(own, beside, across, mine, out, *scratch):
    out[...] = hermite_partial(own, beside, across, [mine], *scratch)


def hermite_kernel(own, beside, across, early, stars, out, *scratch):
    both = early[...] + hermite_partial(own, beside, across, other_chunks(stars), *scratch)
    me = lax.axis_index(NARROW)
    for n in range(N_NARROW):
        owner = me ^ n
        out[owner, :, 0:STARS] = both[:, n * STARS : (n + 1) * STARS]


EARLY_CELLS, BODY_BLOCK, EARLY_BLOCKS = 2, 2, 4
CELL_BLOCKS, STAR_BLOCK, BLOCKS = 14, 14, 22


def by_group(picked):
    lane_group = lax.broadcasted_iota(jnp.int32, picked[0].shape, 1) // GROUPS
    out = []
    for c in range(4):
        plane = picked[c]
        for k in range(4):
            if k != c:
                plane = jnp.where(lane_group == k, pltpu.roll(picked[k], (GROUPS * (k - c)) % LANES, 1), plane)
        out.append(plane)
    return out


def table_rows(x, y, z, m):
    return (x, y, z, m * x, m * y, m * z, m)


def cell_table(chunks, table):
    rows = [[chunk[64 + 8 * half : 72 + 8 * half, :] for half in range(2)] for chunk in chunks]
    parts = [
        jnp.concatenate([pair[k // 2][4 * (k % 2) : 4 * (k % 2) + 4] for pair in rows], axis=0)
        for k in range(4)
    ]
    for row, plane in enumerate(table_rows(*by_group(parts))):
        store_rows(table, 8, row, plane)


def body_table(gpos, gmass, table):
    for half in range(2):
        spot = slice(8 * (BODY_BLOCK + half), 8 * (BODY_BLOCK + half) + 7)
        for side in range(2):
            span = slice(half * PER_BLOCK + side * LANES, half * PER_BLOCK + (side + 1) * LANES)
            m = gmass[:, span]
            table[side, spot, :] = jnp.concatenate([gpos[:, span], gpos[:, span] * m, m], axis=0)


def star_table(leaf_ref, chunks, table, splanes):
    x, y = star_plane_pair(chunks, 0)
    z, _ = star_plane_pair(chunks, 1)
    m, _ = star_plane_pair(chunks, 3)
    me = lax.axis_index(XY)
    for c, plane in enumerate((x, y, z, m)):
        splanes[pl.ds(c, 64, stride=8), :] = plane
    low = low_lanes((8, LANES))
    for leaf in range(4):
        for pair in range(4):
            sides = []
            for side in range(2):
                b = leaf_ref[leaf, 2 * pair + side]
                chunk = lax.rem(b % N_XY - me + (N_XY - 1) + N_XY, N_XY)
                z_at = b // N_XY
                upper = z_at // (N_Z // 2)
                at = chunk * (N_Z // 2) + z_at - upper * (N_Z // 2)
                rows = splanes[pl.ds(pl.multiple_of(at * 8, 8), 8), :]
                sides.append(jnp.where(upper == side, rows, pltpu.roll(rows, 64, 1)))
            rows = jnp.where(low, sides[0], sides[1])
            m = rows[3:4]
            first = 8 * (STAR_BLOCK + 2 * leaf + pair // 2)
            table[pair % 2, first : first + 7, :] = jnp.concatenate(
                [rows[0:3], rows[0:3] * m, m], axis=0
            )


def pull_of(block, here):
    dx, dy, dz = [block[c : c + 1] - here[c] for c in range(3)]
    inv = lax.rsqrt(dx * dx + (dy * dy + (dz * dz + SOFT_SQ)))
    return weighted(block, inv * (inv * inv))


def spread_bodies(gpos, here):
    turned = jnp.transpose(jnp.concatenate([gpos[...], jnp.zeros((5, 4 * LEAF), F32)], axis=0))
    for c in range(3):
        here[c] = jnp.broadcast_to(turned[:, c : c + 1], (4 * LEAF, LANES))


def pull_all_bodies(table, blocks, unroll, here, total):
    half = 2 * LEAF

    def block(b, _):
        g = load_block(table, pl.multiple_of(b * 8, 8))
        for first in (0, half):
            spot = slice(first, first + half)
            total[:, spot] += pull_of(g, [twice(here[c, spot]) for c in range(3)])
        return 0

    lax.fori_loop(0, blocks, block, 0, unroll=unroll)


def body_pull(total, gpos):
    summed = add_parts(total[...])
    return summed[3:6] - gpos[...] * summed[6:7]


def star_pull(own, table, blocks, more):
    turned = jnp.transpose(own[...])
    at = [
        jnp.broadcast_to(turned[64 * (c % 2) : 64 * (c % 2) + 64, c // 2 : c // 2 + 1], (STARS, LANES))
        for c in range(3)
    ]

    def add_pull(source, sums):
        dx, dy, dz = [source[c] - at[c] for c in range(3)]
        inv = lax.rsqrt(dx * dx + (dy * dy + (dz * dz + SOFT_SQ)))
        weight = source[3] * inv * (inv * inv)
        return sums[0] + weight * dx, sums[1] + weight * dy, sums[2] + weight * dz

    def row(b, sums):
        for side in range(2):
            sums = add_pull([table[side, pl.ds(b * 8 + r, 1), :] for r in (0, 1, 2, 6)], sums)
        return sums

    res = (jnp.zeros((STARS, LANES), F32),) * 3
    if more is not None:
        res = add_pull(more, res)
    res = lax.fori_loop(0, blocks, row, res, unroll=2)
    return jnp.concatenate([row_sums(part) for part in res], axis=0)


def early_pull_kernel(gpos, gmass, own, cells, mine, gal_out, cell_out, table, here, total):
    table[...] = jnp.zeros(table.shape, F32)
    cell_table([mine], table)
    body_table(gpos, gmass, table)
    spread_bodies(gpos, here)
    total[...] = jnp.zeros(total.shape, F32)
    pull_all_bodies(table, EARLY_BLOCKS, 2, here, total)
    gal_out[...] = body_pull(total, gpos)
    leaf_cells = by_group([cells[k : k + 1] for k in range(4)])
    cell_out[...] = star_pull(own, table, EARLY_CELLS, leaf_cells)


def pull_kernel(
    leaf_ref, gpos, gvel, stars, own, early_gal, early_cell, gal_out, cell_out, table, splanes, here, total
):
    table[...] = jnp.zeros(table.shape, F32)
    splanes[...] = jnp.zeros(splanes.shape, F32)
    others = other_chunks(stars)
    cell_table(others, table)
    star_table(leaf_ref, others + [stars.at[lax.axis_index(XY)]], table, splanes)
    spread_bodies(gpos, here)
    total[...] = jnp.zeros(total.shape, F32)
    pull_all_bodies(table, CELL_BLOCKS, 2, here, total)
    for leaf in range(4):
        spot = slice(leaf * LEAF, (leaf + 1) * LEAF)
        for k in range(2):
            g = load_block(table, 8 * (STAR_BLOCK + 2 * leaf + k))
            total[:, spot] += pull_of(g, [twice(here[c, spot]) for c in range(3)])
    gal_out[...] = gvel[...] + TIME_STEP * (early_gal[...] + body_pull(total, gpos))
    cell_out[...] = early_cell[...] + star_pull(own, table, CELL_BLOCKS, None)


def correct_kernel(state, parts, cell, pos_out, vel_out):
    pos, vel, acc, jerk = [state[k] for k in range(4)]
    summed = parts[0] + parts[1] + parts[2] + parts[3]
    new_acc = summed[0:3, 0:STARS] + cell[...]
    new_jerk = summed[3:6, 0:STARS]
    new_vel = (
        vel
        + TIME_STEP * 0.5 * (acc + new_acc)
        + STEP_SQ / 12.0 * (jerk - new_jerk)
    )
    vel_out[...] = new_vel
    pos_out[...] = (
        pos
        + TIME_STEP * 0.5 * (vel + new_vel)
        + STEP_SQ / 12.0 * (acc - new_acc)
    )


def shape(*lengths):
    return jax.ShapeDtypeStruct(lengths, F32)


VMEM_SPEC = pl.BlockSpec(memory_space=pltpu.VMEM)


def call(kernel, out_shape, scratch=(), scalars=0, work=0, space=VMEM_SPEC, extra=(), limit=32 * 1024 * 1024):
    def run(*operands):
        return pl.pallas_call(
            kernel,
            out_shape=out_shape,
            in_specs=[pl.BlockSpec(memory_space=pltpu.SMEM)] * scalars + [space] * (len(operands) - scalars),
            out_specs=jax.tree.map(lambda _: VMEM_SPEC, out_shape),
            scratch_shapes=[pltpu.VMEM(lengths, kind) for lengths, kind in scratch] + list(extra),
            compiler_params=pltpu.CompilerParams(vmem_limit_bytes=limit),
            cost_estimate=pl.CostEstimate(flops=work, bytes_accessed=400_000, transcendentals=work // 40),
        )(*operands)

    return run


def exchange(x, axis):
    return lax.all_to_all(x, axis, split_axis=0, concat_axis=0, tiled=True)


def body(
    star_pos, star_vel, star_mass, star_acc, star_jerk, gal_pos, gal_vel, gal_mass, group_of, let_send, star_leaf
):
    masses = gal_mass.reshape(1, -1)
    operands = (
        star_pos,
        star_vel,
        star_acc,
        star_jerk,
        star_mass.reshape(1, -1),
        gal_pos,
        masses,
        group_of.reshape(1, -1),
        let_send.reshape(1, -1),
    )
    own, cells, send, state = call(
        prepare_kernel,
        (shape(8, LANES), shape(8, LANES), shape(N_Z, 8, LANES), shape(4, 3, STARS)),
        [(x.shape, x.dtype) for x in operands],
        space=pl.BlockSpec(memory_space=pltpu.HBM),
        extra=[pltpu.SemaphoreType.DMA((len(operands),))],
        limit=None,
    )(*operands)
    arrived = exchange(send, Z)
    beside = lax.ppermute(own, NARROW, [(n, n ^ 1) for n in range(N_NARROW)])
    across = lax.ppermute(jnp.concatenate([own, beside]), NARROW, [(n, n ^ 2) for n in range(N_NARROW)])
    arrived, beside, across = lax.optimization_barrier((arrived, beside, across))
    onward, mine = call(onward_kernel, (shape(N_XY, 80, LANES), shape(80, LANES)))(
        arrived.reshape(N_Z * 8, LANES)
    )
    stars = exchange(onward, XY)
    n_targets = N_NARROW * STARS
    body_scratch = [((3, 4 * LEAF, LANES), F32), ((32, 4 * LEAF), F32)]
    early_gal, early_cell = call(
        early_pull_kernel,
        (shape(3, 4 * LEAF), shape(3, STARS)),
        [((2, 8 * (EARLY_BLOCKS + 8), LANES), F32), *body_scratch],
        work=15_000_000,
    )(gal_pos, masses, own, cells, mine)

    def hermite_scratch(blocks):
        return [
            ((2, 16 * (blocks + 4), LANES), F32),
            ((n_targets, 64), BF16),
            ((3, n_targets, LANES), F32),
            ((32, n_targets), F32),
            ((3, n_targets, LANES), F32),
        ]

    early = call(early_hermite_kernel, shape(8, n_targets), hermite_scratch(4), work=10_000_000)(
        own, beside, across, mine
    )
    early, early_gal, early_cell, stars = lax.optimization_barrier((early, early_gal, early_cell, stars))
    partial = call(hermite_kernel, shape(N_NARROW, 8, LANES), hermite_scratch(28), work=70_000_000)(
        own, beside, across, early, stars
    )
    shared = exchange(partial, NARROW)
    gal_vel_new, cell_acc = call(
        pull_kernel,
        (shape(3, 4 * LEAF), shape(3, STARS)),
        [((2, 8 * BLOCKS, LANES), F32), ((64 * 8, LANES), F32), *body_scratch],
        scalars=1,
        work=50_000_000,
    )(star_leaf, gal_pos, gal_vel, stars, own, early_gal, early_cell)
    star_pos_new, star_vel_new = call(correct_kernel, (shape(3, STARS), shape(3, STARS)))(
        state, shared, cell_acc
    )
    return gal_vel_new, star_pos_new, star_vel_new


def solution(mesh):
    torus = Mesh(mesh.devices.reshape(N_Z, N_XY, N_NARROW), ALL)
    cols = P(None, ALL)
    return jax.shard_map(
        body,
        mesh=torus,
        in_specs=(
            cols,
            cols,
            P(ALL),
            cols,
            cols,
            cols,
            cols,
            P(ALL),
            P(ALL),
            P(ALL, None, None),
            P(ALL, None),
        ),
        out_specs=(cols, cols, cols),
        check_vma=False,
    )
```

```python
import jax
import jax.numpy as jnp
from jax import lax
from jax.experimental import pallas as pl
from jax.experimental.pallas import tpu as pltpu
from jax.sharding import Mesh
from jax.sharding import PartitionSpec as P

GROUPS = 32
LEAF = 128
LANES = 128
TIME_STEP = 0.25
SOFT_SQ = 0.05
STEP_SQ = TIME_STEP * TIME_STEP
HIGHEST = lax.Precision.HIGHEST
F32, BF16 = jnp.float32, jnp.bfloat16
LANE_BY_LANE = (((1,), (1,)), ((), ()))

Z, XY, NARROW = "wide_z", "wide_xy", "narrow"
ALL = (Z, XY, NARROW)
N_Z, N_XY, N_NARROW = 16, 8, 4
STARS = 64
STAR_ROWS = 4
CHUNK_ROWS = 72
PER_BLOCK = 2 * LANES
CHUNK_BLOCKS = N_Z * STARS // PER_BLOCK


def predict(pos, vel, acc, jerk):
    pred_pos = pos + TIME_STEP * vel + STEP_SQ * 0.5 * acc + STEP_SQ * TIME_STEP / 6.0 * jerk
    pred_vel = vel + TIME_STEP * acc + STEP_SQ * 0.5 * jerk
    return pred_pos, pred_vel


def prepare_kernel(*refs):
    sources, outs, held, done = refs[:9], refs[9:13], refs[13:22], refs[22]
    own_out, cells_out, send_out, state_out = outs
    copies = [pltpu.make_async_copy(sources[k], held[k], done.at[k]) for k in range(9)]
    for copy in copies:
        copy.start()
    for copy in copies:
        copy.wait()
    pos, vel, acc, jerk, mass, gpos, gmass, group, let = held
    for k, ref in enumerate((pos, vel, acc, jerk)):
        state_out[k] = ref[...]
    pred_pos, pred_vel = predict(pos[...], vel[...], acc[...], jerk[...])
    zero = jnp.zeros((1, STARS), F32)
    rows = [
        (pred_pos[0:1], pred_pos[1:2]),
        (pred_pos[2:3], pred_vel[0:1]),
        (pred_vel[1:2], pred_vel[2:3]),
        (mass[...], zero),
    ]
    packed = jnp.concatenate([jnp.concatenate(pair, axis=1) for pair in rows], axis=0)
    own_out[...] = jnp.concatenate([packed, jnp.zeros((4, LANES), F32)], axis=0)
    leaf_rows = []
    for leaf in range(4):
        span = pl.ds(leaf * LEAF, LEAF)
        m = gmass[:, span]
        stacked = jnp.concatenate([gpos[:, span] * m, m, jnp.zeros((4, LEAF), F32)], axis=0)
        onehot = jnp.where(
            lax.broadcasted_iota(jnp.int32, (GROUPS, LEAF), 0) == group[:, span], 1.0, 0.0
        )
        sums = lax.dot_general(stacked, onehot, LANE_BY_LANE, precision=HIGHEST, preferred_element_type=F32)
        total = sums[3:4]
        centre = sums[0:3] / total
        leaf_rows.append(
            jnp.concatenate([centre[0:1], centre[1:2], centre[2:3], total], axis=1)
        )
    cells_out[...] = jnp.concatenate(leaf_rows + [jnp.zeros((4, LANES), F32)], axis=0)
    ids = let[...].astype(F32)
    lane = lax.broadcasted_iota(jnp.int32, (1, LANES), 1)
    listed = jnp.logical_and(lane >= 64, lane < 64 + N_XY)
    for z in range(N_Z):
        turned = pltpu.roll(ids, (64 - N_XY * z) % LANES, 1)
        last = jnp.where(listed, turned, packed[3:4])
        send_out[z] = jnp.concatenate([packed[0:3], last] + leaf_rows, axis=0)


def low_lanes(shape):
    return lax.broadcasted_iota(jnp.int32, shape, 1) < 64


def by_group(picked):
    lane_group = lax.broadcasted_iota(jnp.int32, picked[0].shape, 1) // GROUPS
    out = []
    for c in range(4):
        plane = picked[c]
        for k in range(4):
            if k != c:
                plane = jnp.where(lane_group == k, pltpu.roll(picked[k], (GROUPS * (k - c)) % LANES, 1), plane)
        out.append(plane)
    return out


def onward_kernel(arrived, out, mine):
    for r in range(STAR_ROWS):
        rows = arrived[pl.ds(r, N_Z, stride=8), :]
        first, second = rows[: N_Z // 2], rows[N_Z // 2 :]
        low = low_lanes(first.shape)
        pair = (
            jnp.where(low, first, pltpu.roll(second, 64, 1)),
            jnp.where(low, pltpu.roll(first, 64, 1), second),
        )
        for side in range(2 if r < STAR_ROWS - 1 else 1):
            for e in range(N_XY):
                out[e, 8 * (2 * r + side) : 8 * (2 * r + side) + 8, :] = pair[side]
    ids = arrived[pl.ds(3, N_Z, stride=8), :]
    cells = [arrived[pl.ds(4 + leaf, N_Z, stride=8), :] for leaf in range(4)]
    for e in range(N_XY):
        which = jnp.broadcast_to(ids[:, 64 + e : 65 + e], (N_Z, LANES))
        rows = jnp.zeros((N_Z, LANES), F32)
        for leaf in range(4):
            rows = jnp.where(which == float(leaf), cells[leaf], rows)
        planes = by_group([rows[4 * k : 4 * k + 4] for k in range(4)])
        for half in range(2):
            out[e, 56 + 8 * half : 64 + 8 * half, :] = jnp.concatenate(planes[2 * half : 2 * half + 2], axis=0)
    mine[...] = out[lax.axis_index(XY)]


def star_plane(chunks, c):
    return jnp.concatenate([chunk[8 * c : 8 * c + 8, :] for chunk in chunks], axis=0)


def other_chunks(stars):
    me = lax.axis_index(XY)
    return [stars.at[lax.rem(me + k, N_XY)] for k in range(1, N_XY)]


def row_sums(x):
    ones = jnp.ones((8, LANES), F32)
    return lax.dot_general(ones, x, LANE_BY_LANE, precision=HIGHEST, preferred_element_type=F32)[0:1]


def split3(x):
    high = x.astype(BF16).astype(F32)
    rest = x - high
    middle = rest.astype(BF16).astype(F32)
    return high, middle, rest - middle


def source_slots(x):
    h, m, l = split3(x)
    none = jnp.zeros_like(x)
    return jnp.concatenate([h, h, h, m, m, l, none, none], axis=0).astype(BF16)


def target_slots(x):
    h, m, l = split3(x)
    rows = jnp.concatenate([h, m, l, h, m, h] + [jnp.zeros_like(x)] * 10, axis=0)
    return jnp.transpose(rows)[:, 0:64].astype(BF16)


def weighted(source, weight):
    h, m, l = split3(source)
    parts = jnp.concatenate([h, m, l, jnp.zeros_like(source)], axis=0).astype(BF16)
    high = weight.astype(BF16)
    low = (weight - high.astype(F32)).astype(BF16)
    return lax.dot_general(parts, high, LANE_BY_LANE, preferred_element_type=F32) + lax.dot_general(
        parts, low, LANE_BY_LANE, preferred_element_type=F32
    )


def add_parts(x):
    return x[0:8] + x[8:16] + x[16:24]


def twice(x):
    return jnp.concatenate([x, x], axis=1)


def store_rows(ref, stride, row, plane):
    blocks = plane.shape[0] // 2
    ref[0, pl.ds(row, blocks, stride=stride), :] = plane[:blocks]
    ref[1, pl.ds(row, blocks, stride=stride), :] = plane[blocks:]


def load_block(ref, at):
    return jnp.concatenate([ref[half, pl.ds(at, 8), :] for half in range(2)], axis=1)


def hermite_partial(own, beside, across, chunks, table, slots, here, main, drag):
    n_targets = N_NARROW * STARS
    x, y, z, u, v, w, m = [star_plane(chunks, c) for c in range(7)]
    product = m * (x * u + y * v + z * w)
    for row, plane in enumerate((x, y, z)):
        store_rows(table, 16, row, plane)
    for row, plane in enumerate((m * x, m * y, m * z, m * u, m * v, m * w, m, product)):
        store_rows(table, 16, 8 + row, plane)
    comps = [[] for _ in range(6)]
    for n in range(N_NARROW):
        block = (own[...], beside[...], across[0:8], across[8:16])[n]
        for c in range(6):
            comps[c].append(block[c // 2 : c // 2 + 1, 64 * (c % 2) : 64 * (c % 2) + 64])
    rows = [jnp.concatenate(parts, axis=1) for parts in comps]
    p = jnp.concatenate(rows[0:3], axis=0)
    q = jnp.concatenate(rows[3:6], axis=0)
    own_product = jnp.sum(p * q, axis=0, keepdims=True)
    slots[...] = target_slots(
        jnp.concatenate([-q, -p, own_product, jnp.ones((1, n_targets), F32)], axis=0)
    )
    turned = jnp.transpose(jnp.concatenate([p, jnp.zeros((5, n_targets), F32)], axis=0))
    for c in range(3):
        here[c] = jnp.broadcast_to(turned[:, c : c + 1], (n_targets, LANES))
    main[...] = jnp.zeros(main.shape, F32)
    drag[...] = jnp.zeros(drag.shape, F32)

    def block(b, _):
        at = pl.multiple_of(b * 16, 16)
        g = load_block(table, at)
        s = load_block(table, at + 8)
        dx, dy, dz = [g[c : c + 1] - twice(here[c]) for c in range(3)]
        inv = lax.rsqrt(dx * dx + (dy * dy + (dz * dz + SOFT_SQ)))
        approach = jnp.dot(slots[...], source_slots(s), preferred_element_type=F32)
        inv2 = inv * inv
        weight = inv * inv2
        main[...] += weighted(s, weight)
        pulled = weight * inv2 * approach
        for c, d in enumerate((dx, dy, dz)):
            term = pulled * d
            drag[c] += term[:, 0:LANES] + term[:, LANES:PER_BLOCK]
        return 0

    lax.fori_loop(0, CHUNK_BLOCKS * len(chunks), block, 0, unroll=14 if len(chunks) > 1 else 4)
    total = add_parts(main[...])
    accel = total[0:3] - p * total[6:7]
    dragged = jnp.concatenate([row_sums(drag[c]) for c in range(3)], axis=0)
    jerk = total[3:6] - q * total[6:7] - 3.0 * dragged
    both = jnp.concatenate([accel, jerk, jnp.zeros((2, n_targets), F32)], axis=0)
    return both


def early_hermite_kernel(own, beside, across, mine, out, *scratch):
    out[...] = hermite_partial(own, beside, across, [mine], *scratch)


def hermite_kernel(own, beside, across, early, stars, out, *scratch):
    both = early[...] + hermite_partial(own, beside, across, other_chunks(stars), *scratch)
    me = lax.axis_index(NARROW)
    for n in range(N_NARROW):
        owner = me ^ n
        out[owner, :, 0:STARS] = both[:, n * STARS : (n + 1) * STARS]


EARLY_CELLS, BODY_BLOCK, EARLY_BLOCKS = 2, 2, 4
CELL_BLOCKS, STAR_BLOCK, BLOCKS = 14, 14, 22


def table_rows(x, y, z, m):
    return (x, y, z, m * x, m * y, m * z, m)


def cell_table(chunks, table):
    planes = []
    for c in range(4):
        at = 56 + 8 * (c // 2)
        rows = [chunk[at : at + 8, :][4 * (c % 2) : 4 * (c % 2) + 4] for chunk in chunks]
        planes.append(jnp.concatenate(rows, axis=0))
    for row, plane in enumerate(table_rows(*planes)):
        store_rows(table, 8, row, plane)


def body_table(gpos, gmass, table):
    for half in range(2):
        spot = slice(8 * (BODY_BLOCK + half), 8 * (BODY_BLOCK + half) + 7)
        for side in range(2):
            span = slice(half * PER_BLOCK + side * LANES, half * PER_BLOCK + (side + 1) * LANES)
            m = gmass[:, span]
            table[side, spot, :] = jnp.concatenate([gpos[:, span], gpos[:, span] * m, m], axis=0)


def star_table(leaf_ref, chunks, table, splanes):
    me = lax.axis_index(XY)
    for row, c in enumerate((0, 1, 2, 6)):
        splanes[pl.ds(row, 64, stride=8), :] = star_plane(chunks, c)
    low = low_lanes((8, LANES))
    for leaf in range(4):
        for pair in range(4):
            sides = []
            for side in range(2):
                b = leaf_ref[leaf, 2 * pair + side]
                chunk = lax.rem(b % N_XY - me + (N_XY - 1) + N_XY, N_XY)
                z_at = b // N_XY
                upper = z_at // (N_Z // 2)
                at = chunk * (N_Z // 2) + z_at - upper * (N_Z // 2)
                rows = splanes[pl.ds(pl.multiple_of(at * 8, 8), 8), :]
                sides.append(jnp.where(upper == side, rows, pltpu.roll(rows, 64, 1)))
            rows = jnp.where(low, sides[0], sides[1])
            m = rows[3:4]
            first = 8 * (STAR_BLOCK + 2 * leaf + pair // 2)
            table[pair % 2, first : first + 7, :] = jnp.concatenate(
                [rows[0:3], rows[0:3] * m, m], axis=0
            )


def pull_of(block, here):
    dx, dy, dz = [block[c : c + 1] - here[c] for c in range(3)]
    inv = lax.rsqrt(dx * dx + (dy * dy + (dz * dz + SOFT_SQ)))
    return weighted(block, inv * (inv * inv))


def spread_bodies(gpos, here):
    turned = jnp.transpose(jnp.concatenate([gpos[...], jnp.zeros((5, 4 * LEAF), F32)], axis=0))
    for c in range(3):
        here[c] = jnp.broadcast_to(turned[:, c : c + 1], (4 * LEAF, LANES))


def pull_all_bodies(table, blocks, unroll, here, total):
    half = 2 * LEAF

    def block(b, _):
        g = load_block(table, pl.multiple_of(b * 8, 8))
        for first in (0, half):
            spot = slice(first, first + half)
            total[:, spot] += pull_of(g, [twice(here[c, spot]) for c in range(3)])
        return 0

    lax.fori_loop(0, blocks, block, 0, unroll=unroll)


def body_pull(total, gpos):
    summed = add_parts(total[...])
    return summed[3:6] - gpos[...] * summed[6:7]


def star_pull(own, table, blocks, more):
    turned = jnp.transpose(own[...])
    at = [
        jnp.broadcast_to(turned[64 * (c % 2) : 64 * (c % 2) + 64, c // 2 : c // 2 + 1], (STARS, LANES))
        for c in range(3)
    ]

    def add_pull(source, sums):
        dx, dy, dz = [source[c] - at[c] for c in range(3)]
        inv = lax.rsqrt(dx * dx + (dy * dy + (dz * dz + SOFT_SQ)))
        weight = source[3] * inv * (inv * inv)
        return sums[0] + weight * dx, sums[1] + weight * dy, sums[2] + weight * dz

    def row(b, sums):
        for side in range(2):
            sums = add_pull([table[side, pl.ds(b * 8 + r, 1), :] for r in (0, 1, 2, 6)], sums)
        return sums

    res = (jnp.zeros((STARS, LANES), F32),) * 3
    if more is not None:
        res = add_pull(more, res)
    res = lax.fori_loop(0, blocks, row, res, unroll=blocks)
    return jnp.concatenate([row_sums(part) for part in res], axis=0)


def early_pull_kernel(gpos, gmass, own, cells, mine, gal_out, cell_out, table, here, total):
    table[...] = jnp.zeros(table.shape, F32)
    cell_table([mine], table)
    body_table(gpos, gmass, table)
    spread_bodies(gpos, here)
    total[...] = jnp.zeros(total.shape, F32)
    pull_all_bodies(table, EARLY_BLOCKS, 2, here, total)
    gal_out[...] = body_pull(total, gpos)
    leaf_cells = by_group([cells[k : k + 1] for k in range(4)])
    cell_out[...] = star_pull(own, table, EARLY_CELLS, leaf_cells)


def pull_kernel(
    leaf_ref, gpos, gvel, stars, own, early_gal, early_cell, gal_out, cell_out, table, splanes, here, total
):
    table[...] = jnp.zeros(table.shape, F32)
    splanes[...] = jnp.zeros(splanes.shape, F32)
    others = other_chunks(stars)
    cell_table(others, table)
    star_table(leaf_ref, others + [stars.at[lax.axis_index(XY)]], table, splanes)
    spread_bodies(gpos, here)
    total[...] = jnp.zeros(total.shape, F32)
    pull_all_bodies(table, CELL_BLOCKS, CELL_BLOCKS, here, total)
    for leaf in range(4):
        spot = slice(leaf * LEAF, (leaf + 1) * LEAF)
        for k in range(2):
            g = load_block(table, 8 * (STAR_BLOCK + 2 * leaf + k))
            total[:, spot] += pull_of(g, [twice(here[c, spot]) for c in range(3)])
    gal_out[...] = gvel[...] + TIME_STEP * (early_gal[...] + body_pull(total, gpos))
    cell_out[...] = early_cell[...] + star_pull(own, table, CELL_BLOCKS, None)


def correct_kernel(state, parts, cell, pos_out, vel_out):
    pos, vel, acc, jerk = [state[k] for k in range(4)]
    summed = parts[0] + parts[1] + parts[2] + parts[3]
    new_acc = summed[0:3, 0:STARS] + cell[...]
    new_jerk = summed[3:6, 0:STARS]
    new_vel = (
        vel
        + TIME_STEP * 0.5 * (acc + new_acc)
        + STEP_SQ / 12.0 * (jerk - new_jerk)
    )
    vel_out[...] = new_vel
    pos_out[...] = (
        pos
        + TIME_STEP * 0.5 * (vel + new_vel)
        + STEP_SQ / 12.0 * (acc - new_acc)
    )


def shape(*lengths):
    return jax.ShapeDtypeStruct(lengths, F32)


VMEM_SPEC = pl.BlockSpec(memory_space=pltpu.VMEM)


def call(kernel, out_shape, scratch=(), scalars=0, work=0, space=VMEM_SPEC, extra=(), limit=32 * 1024 * 1024):
    def run(*operands):
        return pl.pallas_call(
            kernel,
            out_shape=out_shape,
            in_specs=[pl.BlockSpec(memory_space=pltpu.SMEM)] * scalars + [space] * (len(operands) - scalars),
            out_specs=jax.tree.map(lambda _: VMEM_SPEC, out_shape),
            scratch_shapes=[pltpu.VMEM(lengths, kind) for lengths, kind in scratch] + list(extra),
            compiler_params=pltpu.CompilerParams(vmem_limit_bytes=limit),
            cost_estimate=pl.CostEstimate(flops=work, bytes_accessed=400_000, transcendentals=work // 40),
        )(*operands)

    return run


def exchange(x, axis):
    return lax.all_to_all(x, axis, split_axis=0, concat_axis=0, tiled=True)


def body(
    star_pos, star_vel, star_mass, star_acc, star_jerk, gal_pos, gal_vel, gal_mass, group_of, let_send, star_leaf
):
    masses = gal_mass.reshape(1, -1)
    operands = (
        star_pos,
        star_vel,
        star_acc,
        star_jerk,
        star_mass.reshape(1, -1),
        gal_pos,
        masses,
        group_of.reshape(1, -1),
        let_send.reshape(1, -1),
    )
    own, cells, send, state = call(
        prepare_kernel,
        (shape(8, LANES), shape(8, LANES), shape(N_Z, 8, LANES), shape(4, 3, STARS)),
        [(x.shape, x.dtype) for x in operands],
        space=pl.BlockSpec(memory_space=pltpu.HBM),
        extra=[pltpu.SemaphoreType.DMA((len(operands),))],
        limit=None,
    )(*operands)
    arrived = exchange(send, Z)
    beside = lax.ppermute(own, NARROW, [(n, n ^ 1) for n in range(N_NARROW)])
    across = lax.ppermute(jnp.concatenate([own, beside]), NARROW, [(n, n ^ 2) for n in range(N_NARROW)])
    arrived, beside, across = lax.optimization_barrier((arrived, beside, across))
    onward, mine = call(onward_kernel, (shape(N_XY, CHUNK_ROWS, LANES), shape(CHUNK_ROWS, LANES)))(
        arrived.reshape(N_Z * 8, LANES)
    )
    stars = exchange(onward, XY)
    n_targets = N_NARROW * STARS
    body_scratch = [((3, 4 * LEAF, LANES), F32), ((32, 4 * LEAF), F32)]
    early_gal, early_cell = call(
        early_pull_kernel,
        (shape(3, 4 * LEAF), shape(3, STARS)),
        [((2, 8 * (EARLY_BLOCKS + 8), LANES), F32), *body_scratch],
        work=15_000_000,
    )(gal_pos, masses, own, cells, mine)

    def hermite_scratch(blocks):
        return [
            ((2, 16 * (blocks + 4), LANES), F32),
            ((n_targets, 64), BF16),
            ((3, n_targets, LANES), F32),
            ((32, n_targets), F32),
            ((3, n_targets, LANES), F32),
        ]

    early = call(early_hermite_kernel, shape(8, n_targets), hermite_scratch(4), work=10_000_000)(
        own, beside, across, mine
    )
    early, early_gal, early_cell, stars = lax.optimization_barrier((early, early_gal, early_cell, stars))
    partial = call(hermite_kernel, shape(N_NARROW, 8, LANES), hermite_scratch(28), work=70_000_000)(
        own, beside, across, early, stars
    )
    shared = exchange(partial, NARROW)
    gal_vel_new, cell_acc = call(
        pull_kernel,
        (shape(3, 4 * LEAF), shape(3, STARS)),
        [((2, 8 * BLOCKS, LANES), F32), ((64 * 8, LANES), F32), *body_scratch],
        scalars=1,
        work=50_000_000,
    )(star_leaf, gal_pos, gal_vel, stars, own, early_gal, early_cell)
    star_pos_new, star_vel_new = call(correct_kernel, (shape(3, STARS), shape(3, STARS)))(
        state, shared, cell_acc
    )
    return gal_vel_new, star_pos_new, star_vel_new


def solution(mesh):
    torus = Mesh(mesh.devices.reshape(N_Z, N_XY, N_NARROW), ALL)
    cols = P(None, ALL)
    return jax.shard_map(
        body,
        mesh=torus,
        in_specs=(
            cols,
            cols,
            P(ALL),
            cols,
            cols,
            cols,
            cols,
            P(ALL),
            P(ALL),
            P(ALL, None, None),
            P(ALL, None),
        ),
        out_specs=(cols, cols, cols),
        check_vma=False,
    )
```

```python
import jax
import jax.numpy as jnp
from jax import lax
from jax.experimental import pallas as pl
from jax.experimental.pallas import tpu as pltpu
from jax.sharding import Mesh
from jax.sharding import PartitionSpec as P

GROUPS = 32
LEAF = 128
LANES = 128
TIME_STEP = 0.25
SOFT_SQ = 0.05
STEP_SQ = TIME_STEP * TIME_STEP
HIGHEST = lax.Precision.HIGHEST
F32, BF16 = jnp.float32, jnp.bfloat16
LANE_BY_LANE = (((1,), (1,)), ((), ()))

Z, XY, NARROW = "wide_z", "wide_xy", "narrow"
ALL = (Z, XY, NARROW)
N_Z, N_XY, N_NARROW = 16, 8, 4
STARS = 64
STAR_ROWS = 4
CHUNK_ROWS = 72
PER_BLOCK = 2 * LANES
CHUNK_BLOCKS = N_Z * STARS // PER_BLOCK


def predict(pos, vel, acc, jerk):
    pred_pos = pos + TIME_STEP * vel + STEP_SQ * 0.5 * acc + STEP_SQ * TIME_STEP / 6.0 * jerk
    pred_vel = vel + TIME_STEP * acc + STEP_SQ * 0.5 * jerk
    return pred_pos, pred_vel


def prepare_kernel(*refs):
    sources, outs, held, done = refs[:9], refs[9:13], refs[13:22], refs[22]
    own_out, cells_out, send_out, state_out = outs
    copies = [pltpu.make_async_copy(sources[k], held[k], done.at[k]) for k in range(9)]
    for copy in copies:
        copy.start()
    for copy in copies:
        copy.wait()
    pos, vel, acc, jerk, mass, gpos, gmass, group, let = held
    for k, ref in enumerate((pos, vel, acc, jerk)):
        state_out[k] = ref[...]
    pred_pos, pred_vel = predict(pos[...], vel[...], acc[...], jerk[...])
    zero = jnp.zeros((1, STARS), F32)
    rows = [
        (pred_pos[0:1], pred_pos[1:2]),
        (pred_pos[2:3], pred_vel[0:1]),
        (pred_vel[1:2], pred_vel[2:3]),
        (mass[...], zero),
    ]
    packed = jnp.concatenate([jnp.concatenate(pair, axis=1) for pair in rows], axis=0)
    own_out[...] = jnp.concatenate([packed, jnp.zeros((4, LANES), F32)], axis=0)
    leaf_rows = []
    for leaf in range(4):
        span = pl.ds(leaf * LEAF, LEAF)
        m = gmass[:, span]
        stacked = jnp.concatenate([gpos[:, span] * m, m, jnp.zeros((4, LEAF), F32)], axis=0)
        onehot = jnp.where(
            lax.broadcasted_iota(jnp.int32, (GROUPS, LEAF), 0) == group[:, span], 1.0, 0.0
        )
        sums = lax.dot_general(stacked, onehot, LANE_BY_LANE, precision=HIGHEST, preferred_element_type=F32)
        total = sums[3:4]
        centre = sums[0:3] / total
        leaf_rows.append(
            jnp.concatenate([centre[0:1], centre[1:2], centre[2:3], total], axis=1)
        )
    cells_out[...] = jnp.concatenate(leaf_rows + [jnp.zeros((4, LANES), F32)], axis=0)
    ids = let[...].astype(F32)
    lane = lax.broadcasted_iota(jnp.int32, (1, LANES), 1)
    listed = jnp.logical_and(lane >= 64, lane < 64 + N_XY)
    for z in range(N_Z):
        turned = pltpu.roll(ids, (64 - N_XY * z) % LANES, 1)
        last = jnp.where(listed, turned, packed[3:4])
        send_out[z] = jnp.concatenate([packed[0:3], last] + leaf_rows, axis=0)


def low_lanes(shape):
    return lax.broadcasted_iota(jnp.int32, shape, 1) < 64


def by_group(picked):
    lane_group = lax.broadcasted_iota(jnp.int32, picked[0].shape, 1) // GROUPS
    out = []
    for c in range(4):
        plane = picked[c]
        for k in range(4):
            if k != c:
                plane = jnp.where(lane_group == k, pltpu.roll(picked[k], (GROUPS * (k - c)) % LANES, 1), plane)
        out.append(plane)
    return out


def onward_kernel(arrived, out, mine):
    for r in range(STAR_ROWS):
        rows = arrived[pl.ds(r, N_Z, stride=8), :]
        first, second = rows[: N_Z // 2], rows[N_Z // 2 :]
        low = low_lanes(first.shape)
        pair = (
            jnp.where(low, first, pltpu.roll(second, 64, 1)),
            jnp.where(low, pltpu.roll(first, 64, 1), second),
        )
        for side in range(2 if r < STAR_ROWS - 1 else 1):
            for e in range(N_XY):
                out[e, 8 * (2 * r + side) : 8 * (2 * r + side) + 8, :] = pair[side]
    ids = arrived[pl.ds(3, N_Z, stride=8), :]
    cells = [arrived[pl.ds(4 + leaf, N_Z, stride=8), :] for leaf in range(4)]
    for e in range(N_XY):
        which = jnp.broadcast_to(ids[:, 64 + e : 65 + e], (N_Z, LANES))
        rows = jnp.zeros((N_Z, LANES), F32)
        for leaf in range(4):
            rows = jnp.where(which == float(leaf), cells[leaf], rows)
        planes = by_group([rows[4 * k : 4 * k + 4] for k in range(4)])
        for half in range(2):
            out[e, 56 + 8 * half : 64 + 8 * half, :] = jnp.concatenate(planes[2 * half : 2 * half + 2], axis=0)
    mine[...] = out[lax.axis_index(XY)]


def star_plane(chunks, c):
    return jnp.concatenate([chunk[8 * c : 8 * c + 8, :] for chunk in chunks], axis=0)


def other_chunks(stars):
    me = lax.axis_index(XY)
    return [stars.at[lax.rem(me + k, N_XY)] for k in range(1, N_XY)]


def row_sums(x):
    ones = jnp.ones((8, LANES), F32)
    return lax.dot_general(ones, x, LANE_BY_LANE, precision=HIGHEST, preferred_element_type=F32)[0:1]


def split3(x):
    high = x.astype(BF16).astype(F32)
    rest = x - high
    middle = rest.astype(BF16).astype(F32)
    return high, middle, rest - middle


def source_slots(x):
    h, m, l = split3(x)
    none = jnp.zeros_like(x)
    return jnp.concatenate([h, h, h, m, m, l, none, none], axis=0).astype(BF16)


def target_slots(x):
    h, m, l = split3(x)
    rows = jnp.concatenate([h, m, l, h, m, h] + [jnp.zeros_like(x)] * 10, axis=0)
    return jnp.transpose(rows)[:, 0:64].astype(BF16)


def weighted(source, weight):
    h, m, l = split3(source)
    parts = jnp.concatenate([h, m, l, jnp.zeros_like(source)], axis=0).astype(BF16)
    high = weight.astype(BF16)
    low = (weight - high.astype(F32)).astype(BF16)
    return lax.dot_general(parts, high, LANE_BY_LANE, preferred_element_type=F32) + lax.dot_general(
        parts, low, LANE_BY_LANE, preferred_element_type=F32
    )


def add_parts(x):
    return x[0:8] + x[8:16] + x[16:24]


def twice(x):
    return jnp.concatenate([x, x], axis=1)


def store_rows(ref, stride, row, plane):
    blocks = plane.shape[0] // 2
    ref[0, pl.ds(row, blocks, stride=stride), :] = plane[:blocks]
    ref[1, pl.ds(row, blocks, stride=stride), :] = plane[blocks:]


def load_block(ref, at):
    return jnp.concatenate([ref[half, pl.ds(at, 8), :] for half in range(2)], axis=1)


def hermite_partial(own, beside, across, chunks, table, slots, here, main, drag, spread):
    n_targets = N_NARROW * STARS
    x, y, z, u, v, w, m = [star_plane(chunks, c) for c in range(7)]
    product = m * (x * u + y * v + z * w)
    for row, plane in enumerate((x, y, z)):
        store_rows(table, 16, row, plane)
    for row, plane in enumerate((m * x, m * y, m * z, m * u, m * v, m * w, m, product)):
        store_rows(table, 16, 8 + row, plane)
    comps = [[] for _ in range(6)]
    for n in range(N_NARROW):
        block = (own[...], beside[...], across[0:8], across[8:16])[n]
        for c in range(6):
            comps[c].append(block[c // 2 : c // 2 + 1, 64 * (c % 2) : 64 * (c % 2) + 64])
    rows = [jnp.concatenate(parts, axis=1) for parts in comps]
    p = jnp.concatenate(rows[0:3], axis=0)
    q = jnp.concatenate(rows[3:6], axis=0)
    own_product = jnp.sum(p * q, axis=0, keepdims=True)
    if spread:
        slots[...] = target_slots(
            jnp.concatenate([-q, -p, own_product, jnp.ones((1, n_targets), F32)], axis=0)
        )
        turned = jnp.transpose(jnp.concatenate([p, jnp.zeros((5, n_targets), F32)], axis=0))
        for c in range(3):
            here[c] = jnp.broadcast_to(turned[:, c : c + 1], (n_targets, LANES))
    main[...] = jnp.zeros(main.shape, F32)
    drag[...] = jnp.zeros(drag.shape, F32)

    def block(b, _):
        at = pl.multiple_of(b * 16, 16)
        g = load_block(table, at)
        s = load_block(table, at + 8)
        dx, dy, dz = [g[c : c + 1] - twice(here[c]) for c in range(3)]
        inv = lax.rsqrt(dx * dx + (dy * dy + (dz * dz + SOFT_SQ)))
        approach = jnp.dot(slots[...], source_slots(s), preferred_element_type=F32)
        inv2 = inv * inv
        weight = inv * inv2
        main[...] += weighted(s, weight)
        pulled = weight * inv2 * approach
        for c, d in enumerate((dx, dy, dz)):
            term = pulled * d
            drag[c] += term[:, 0:LANES] + term[:, LANES:PER_BLOCK]
        return 0

    lax.fori_loop(0, CHUNK_BLOCKS * len(chunks), block, 0, unroll=14 if len(chunks) > 1 else 4)
    total = add_parts(main[...])
    accel = total[0:3] - p * total[6:7]
    dragged = jnp.concatenate([row_sums(drag[c]) for c in range(3)], axis=0)
    jerk = total[3:6] - q * total[6:7] - 3.0 * dragged
    both = jnp.concatenate([accel, jerk, jnp.zeros((2, n_targets), F32)], axis=0)
    return both


def early_hermite_kernel(own, beside, across, mine, out, slots, here, table, main, drag):
    out[...] = hermite_partial(own, beside, across, [mine], table, slots, here, main, drag, True)


def hermite_kernel(own, beside, across, early, slots, here, stars, out, table, main, drag):
    chunks = other_chunks(stars)
    both = early[...] + hermite_partial(own, beside, across, chunks, table, slots, here, main, drag, False)
    me = lax.axis_index(NARROW)
    for n in range(N_NARROW):
        owner = me ^ n
        out[owner, :, 0:STARS] = both[:, n * STARS : (n + 1) * STARS]


EARLY_CELLS, BODY_BLOCK, EARLY_BLOCKS = 2, 2, 4
CELL_BLOCKS, STAR_BLOCK, BLOCKS = 14, 14, 22


def table_rows(x, y, z, m):
    return (x, y, z, m * x, m * y, m * z, m)


def cell_table(chunks, table):
    planes = []
    for c in range(4):
        at = 56 + 8 * (c // 2)
        rows = [chunk[at : at + 8, :][4 * (c % 2) : 4 * (c % 2) + 4] for chunk in chunks]
        planes.append(jnp.concatenate(rows, axis=0))
    for row, plane in enumerate(table_rows(*planes)):
        store_rows(table, 8, row, plane)


def body_table(gpos, gmass, table):
    for half in range(2):
        spot = slice(8 * (BODY_BLOCK + half), 8 * (BODY_BLOCK + half) + 7)
        for side in range(2):
            span = slice(half * PER_BLOCK + side * LANES, half * PER_BLOCK + (side + 1) * LANES)
            m = gmass[:, span]
            table[side, spot, :] = jnp.concatenate([gpos[:, span], gpos[:, span] * m, m], axis=0)


def star_table(leaf_ref, chunks, table, splanes):
    me = lax.axis_index(XY)
    for row, c in enumerate((0, 1, 2, 6)):
        splanes[pl.ds(row, 64, stride=8), :] = star_plane(chunks, c)
    low = low_lanes((8, LANES))
    for leaf in range(4):
        for pair in range(4):
            sides = []
            for side in range(2):
                b = leaf_ref[leaf, 2 * pair + side]
                chunk = lax.rem(b % N_XY - me + (N_XY - 1) + N_XY, N_XY)
                z_at = b // N_XY
                upper = z_at // (N_Z // 2)
                at = chunk * (N_Z // 2) + z_at - upper * (N_Z // 2)
                rows = splanes[pl.ds(pl.multiple_of(at * 8, 8), 8), :]
                sides.append(jnp.where(upper == side, rows, pltpu.roll(rows, 64, 1)))
            rows = jnp.where(low, sides[0], sides[1])
            m = rows[3:4]
            first = 8 * (STAR_BLOCK + 2 * leaf + pair // 2)
            table[pair % 2, first : first + 7, :] = jnp.concatenate(
                [rows[0:3], rows[0:3] * m, m], axis=0
            )


def pull_of(block, here):
    dx, dy, dz = [block[c : c + 1] - here[c] for c in range(3)]
    inv = lax.rsqrt(dx * dx + (dy * dy + (dz * dz + SOFT_SQ)))
    return weighted(block, inv * (inv * inv))


def spread_bodies(gpos, here):
    turned = jnp.transpose(jnp.concatenate([gpos[...], jnp.zeros((5, 4 * LEAF), F32)], axis=0))
    for c in range(3):
        here[c] = jnp.broadcast_to(turned[:, c : c + 1], (4 * LEAF, LANES))


def pull_all_bodies(table, blocks, unroll, here, total):
    half = 2 * LEAF

    def block(b, _):
        g = load_block(table, pl.multiple_of(b * 8, 8))
        for first in (0, half):
            spot = slice(first, first + half)
            total[:, spot] += pull_of(g, [twice(here[c, spot]) for c in range(3)])
        return 0

    lax.fori_loop(0, blocks, block, 0, unroll=unroll)


def body_pull(total, gpos):
    summed = add_parts(total[...])
    return summed[3:6] - gpos[...] * summed[6:7]


def star_pull(own, table, blocks, more):
    turned = jnp.transpose(own[...])
    at = [
        jnp.broadcast_to(turned[64 * (c % 2) : 64 * (c % 2) + 64, c // 2 : c // 2 + 1], (STARS, LANES))
        for c in range(3)
    ]

    def add_pull(source, sums):
        dx, dy, dz = [source[c] - at[c] for c in range(3)]
        inv = lax.rsqrt(dx * dx + (dy * dy + (dz * dz + SOFT_SQ)))
        weight = source[3] * inv * (inv * inv)
        return sums[0] + weight * dx, sums[1] + weight * dy, sums[2] + weight * dz

    def row(b, sums):
        for side in range(2):
            sums = add_pull([table[side, pl.ds(b * 8 + r, 1), :] for r in (0, 1, 2, 6)], sums)
        return sums

    res = (jnp.zeros((STARS, LANES), F32),) * 3
    if more is not None:
        res = add_pull(more, res)
    res = lax.fori_loop(0, blocks, row, res, unroll=blocks)
    return jnp.concatenate([row_sums(part) for part in res], axis=0)


def early_pull_kernel(gpos, gmass, own, cells, mine, gal_out, cell_out, here, table, total):
    table[...] = jnp.zeros(table.shape, F32)
    cell_table([mine], table)
    body_table(gpos, gmass, table)
    spread_bodies(gpos, here)
    total[...] = jnp.zeros(total.shape, F32)
    pull_all_bodies(table, EARLY_BLOCKS, 2, here, total)
    gal_out[...] = body_pull(total, gpos)
    leaf_cells = by_group([cells[k : k + 1] for k in range(4)])
    cell_out[...] = star_pull(own, table, EARLY_CELLS, leaf_cells)


def pull_kernel(
    leaf_ref, gpos, gvel, stars, own, early_gal, early_cell, here, gal_out, cell_out, table, splanes, total
):
    table[...] = jnp.zeros(table.shape, F32)
    splanes[...] = jnp.zeros(splanes.shape, F32)
    others = other_chunks(stars)
    cell_table(others, table)
    star_table(leaf_ref, others + [stars.at[lax.axis_index(XY)]], table, splanes)
    total[...] = jnp.zeros(total.shape, F32)
    pull_all_bodies(table, CELL_BLOCKS, CELL_BLOCKS, here, total)
    for leaf in range(4):
        spot = slice(leaf * LEAF, (leaf + 1) * LEAF)
        for k in range(2):
            g = load_block(table, 8 * (STAR_BLOCK + 2 * leaf + k))
            total[:, spot] += pull_of(g, [twice(here[c, spot]) for c in range(3)])
    gal_out[...] = gvel[...] + TIME_STEP * (early_gal[...] + body_pull(total, gpos))
    cell_out[...] = early_cell[...] + star_pull(own, table, CELL_BLOCKS, None)


def correct_kernel(state, parts, cell, pos_out, vel_out):
    pos, vel, acc, jerk = [state[k] for k in range(4)]
    summed = parts[0] + parts[1] + parts[2] + parts[3]
    new_acc = summed[0:3, 0:STARS] + cell[...]
    new_jerk = summed[3:6, 0:STARS]
    new_vel = (
        vel
        + TIME_STEP * 0.5 * (acc + new_acc)
        + STEP_SQ / 12.0 * (jerk - new_jerk)
    )
    vel_out[...] = new_vel
    pos_out[...] = (
        pos
        + TIME_STEP * 0.5 * (vel + new_vel)
        + STEP_SQ / 12.0 * (acc - new_acc)
    )


def shape(*lengths):
    return jax.ShapeDtypeStruct(lengths, F32)


VMEM_SPEC = pl.BlockSpec(memory_space=pltpu.VMEM)


def call(kernel, out_shape, scratch=(), scalars=0, work=0, space=VMEM_SPEC, extra=(), limit=32 * 1024 * 1024):
    def run(*operands):
        return pl.pallas_call(
            kernel,
            out_shape=out_shape,
            in_specs=[pl.BlockSpec(memory_space=pltpu.SMEM)] * scalars + [space] * (len(operands) - scalars),
            out_specs=jax.tree.map(lambda _: VMEM_SPEC, out_shape),
            scratch_shapes=[pltpu.VMEM(lengths, kind) for lengths, kind in scratch] + list(extra),
            compiler_params=pltpu.CompilerParams(vmem_limit_bytes=limit),
            cost_estimate=pl.CostEstimate(flops=work, bytes_accessed=400_000, transcendentals=work // 40),
        )(*operands)

    return run


def exchange(x, axis):
    return lax.all_to_all(x, axis, split_axis=0, concat_axis=0, tiled=True)


def body(
    star_pos, star_vel, star_mass, star_acc, star_jerk, gal_pos, gal_vel, gal_mass, group_of, let_send, star_leaf
):
    masses = gal_mass.reshape(1, -1)
    operands = (
        star_pos,
        star_vel,
        star_acc,
        star_jerk,
        star_mass.reshape(1, -1),
        gal_pos,
        masses,
        group_of.reshape(1, -1),
        let_send.reshape(1, -1),
    )
    own, cells, send, state = call(
        prepare_kernel,
        (shape(8, LANES), shape(8, LANES), shape(N_Z, 8, LANES), shape(4, 3, STARS)),
        [(x.shape, x.dtype) for x in operands],
        space=pl.BlockSpec(memory_space=pltpu.HBM),
        extra=[pltpu.SemaphoreType.DMA((len(operands),))],
        limit=None,
    )(*operands)
    arrived = exchange(send, Z)
    beside = lax.ppermute(own, NARROW, [(n, n ^ 1) for n in range(N_NARROW)])
    across = lax.ppermute(jnp.concatenate([own, beside]), NARROW, [(n, n ^ 2) for n in range(N_NARROW)])
    arrived, beside, across = lax.optimization_barrier((arrived, beside, across))
    onward, mine = call(onward_kernel, (shape(N_XY, CHUNK_ROWS, LANES), shape(CHUNK_ROWS, LANES)))(
        arrived.reshape(N_Z * 8, LANES)
    )
    stars = exchange(onward, XY)
    n_targets = N_NARROW * STARS
    body_total = ((32, 4 * LEAF), F32)
    early_gal, early_cell, bodies = call(
        early_pull_kernel,
        (shape(3, 4 * LEAF), shape(3, STARS), shape(3, 4 * LEAF, LANES)),
        [((2, 8 * (EARLY_BLOCKS + 8), LANES), F32), body_total],
        work=15_000_000,
    )(gal_pos, masses, own, cells, mine)

    def hermite_scratch(blocks):
        return [
            ((2, 16 * (blocks + 4), LANES), F32),
            ((32, n_targets), F32),
            ((3, n_targets, LANES), F32),
        ]

    early_shapes = (
        shape(8, n_targets),
        jax.ShapeDtypeStruct((n_targets, 64), BF16),
        shape(3, n_targets, LANES),
    )
    early, slots, targets = call(early_hermite_kernel, early_shapes, hermite_scratch(4), work=10_000_000)(
        own, beside, across, mine
    )
    early, early_gal, early_cell, stars = lax.optimization_barrier((early, early_gal, early_cell, stars))
    partial = call(hermite_kernel, shape(N_NARROW, 8, LANES), hermite_scratch(28), work=70_000_000)(
        own, beside, across, early, slots, targets, stars
    )
    shared = exchange(partial, NARROW)
    gal_vel_new, cell_acc = call(
        pull_kernel,
        (shape(3, 4 * LEAF), shape(3, STARS)),
        [((2, 8 * BLOCKS, LANES), F32), ((64 * 8, LANES), F32), body_total],
        scalars=1,
        work=50_000_000,
    )(star_leaf, gal_pos, gal_vel, stars, own, early_gal, early_cell, bodies)
    star_pos_new, star_vel_new = call(correct_kernel, (shape(3, STARS), shape(3, STARS)))(
        state, shared, cell_acc
    )
    return gal_vel_new, star_pos_new, star_vel_new


def solution(mesh):
    torus = Mesh(mesh.devices.reshape(N_Z, N_XY, N_NARROW), ALL)
    cols = P(None, ALL)
    return jax.shard_map(
        body,
        mesh=torus,
        in_specs=(
            cols,
            cols,
            P(ALL),
            cols,
            cols,
            cols,
            cols,
            P(ALL),
            P(ALL),
            P(ALL, None, None),
            P(ALL, None),
        ),
        out_specs=(cols, cols, cols),
        check_vma=False,
    )
```
